256 devices in a mesh: chan: 4 (over y), ctx: 64 (over z, x, core).
Axes of the slice: x: 4, y: 4, z: 8, core: 2. Of those that a mesh axis runs over, the one named last changes fastest.
Arguments:
- streams: bfloat16 [3, 8192, 8192], P(None, 'ctx', 'chan'), may hold values from -6 to 6
- short_filter: float32 [3, 3, 8192], P(None, None, 'chan'), may hold values from -3 to 3
- rates: float32 [16, 8192], P(None, 'chan'), may hold values from 6.1035156e-05 to 0.03
- residues: float32 [16, 8192], P(None, 'chan'), may hold values from -0.03 to 0.03
- skip: float32 [8192], P('chan'), may hold values from 0.5 to 1.5
Outputs:
- mixed: bfloat16 [8192, 8192], P('ctx', 'chan')
The draws below stay inside these ranges and needn't reach their ends.
All inputs are finite; a program needn't handle non-finite values.
Results may differ from the reference program's by a relative error of at most 0.009.
Values may be sent and summed in bfloat16 or wider, within the bound.
A program may use at most 128 MiB of HBM per device.

```python
import math
import jax
import jax.numpy as jnp
from jax import lax

KERNEL = 3
MODES = 16
CH = 8192
SEQ = 8192


def steps_of(own_key, extent, pieces, smallest, high):
    def one(axis_at, shards_of):
        draws = jax.random.uniform(jax.random.fold_in(jax.random.fold_in(own_key, 6), axis_at), (shards_of,), jnp.float32, smallest / len(pieces), high / len(pieces))
        return jnp.repeat(jnp.exp(draws), extent[axis_at] // shards_of).reshape((-1,) + (1,) * (len(extent) - axis_at - 1))

    loudness = one(*pieces[0])
    for cut in pieces[1:]:
        loudness = loudness * one(*cut)
    return loudness


def noise(rng, dims, spread, most, split=(), kind=jnp.bfloat16):
    entries = spread * jax.random.normal(rng, dims, jnp.float32)
    if split:
        entries = entries * steps_of(rng, dims, split, -0.22, 0.18)
    return jnp.clip(entries, -most, most).astype(kind)


def setup_inputs(seed: int = 0) -> dict:
    arg_keys = jax.random.split(jax.random.key(seed), 6)
    return {
        "streams": noise(arg_keys[0], (3, SEQ, CH), 1.0, 6.0, ((1, 64), (2, 4))),
        "short_filter": noise(arg_keys[1], (KERNEL, 3, CH), 0.6, 3.0, ((2, 4),), jnp.float32),
        "rates": jnp.clip(jnp.exp(math.log(0.03) - 6.1975026 * jax.random.uniform(arg_keys[2], (MODES, CH), jnp.float32) ** steps_of(arg_keys[2], (MODES, CH), ((1, 4),), -0.2, 0.2)), 6.103515625e-05, 0.03),
        "residues": noise(arg_keys[3], (MODES, CH), 0.005, 0.03, ((1, 4),), jnp.float32),
        "skip": jnp.clip(0.5 + 1.0 * jax.random.uniform(arg_keys[4], (CH,), jnp.float32) ** steps_of(arg_keys[4], (CH,), ((0, 4),), -0.2, 0.2), 0.5, 1.5),
    }


def reference(streams, short_filter, rates, residues, skip):
    tap_count = short_filter.shape[0]
    zeros_front = jnp.zeros((3, tap_count - 1, CH), streams.dtype)
    joined = jnp.concatenate([zeros_front, streams], axis=1).astype(jnp.float32)
    features = jnp.zeros((3, SEQ, CH), jnp.float32)
    for lag_index in range(tap_count):
        offset = tap_count - 1 - lag_index
        features = features + short_filter[lag_index][:, None, :] * joined[:, offset:offset + SEQ, :]
    signal = features[1] * features[2]
    positions = jnp.arange(SEQ, dtype=jnp.float32)
    block_width = 128

    def one_block(block_index):
        first_channel = (block_index * block_width).astype(jnp.int32)
        part_signal = lax.dynamic_slice_in_dim(signal, first_channel, block_width, 1)
        part_rates = lax.dynamic_slice_in_dim(rates, first_channel, block_width, 1)
        part_residues = lax.dynamic_slice_in_dim(residues, first_channel, block_width, 1)
        response = jnp.zeros((SEQ, block_width), jnp.float32)
        for mode_index in range(MODES):
            response = response + part_residues[mode_index][None, :] * jnp.exp(-part_rates[mode_index][None, :] * positions[:, None])
        spectrum_signal = jnp.fft.rfft(part_signal, n=2 * SEQ, axis=0)
        spectrum_filter = jnp.fft.rfft(response, n=2 * SEQ, axis=0)
        return jnp.fft.irfft(spectrum_signal * spectrum_filter, n=2 * SEQ, axis=0)[:SEQ].astype(jnp.float32)

    convolved = lax.map(one_block, jnp.arange(CH // block_width, dtype=jnp.int32))
    convolved = jnp.transpose(convolved, (1, 0, 2)).reshape(SEQ, CH)
    mixed_out = features[0] * (convolved + skip[None, :] * signal)
    return mixed_out.astype(jnp.bfloat16)
```

```python
import jax
import jax.numpy as jnp
from jax import lax
from jax.experimental import pallas as pl
from jax.experimental.pallas import tpu as pltpu
from jax.sharding import PartitionSpec as P

MESH = pl.DeviceIdType.MESH
LANES = 128
SUB = 8
GROUP = 8
F32 = jnp.float32
BF16 = jnp.bfloat16


def lanes(index, width=LANES):
    return pl.ds(pl.multiple_of(index * width, width), width)


def gather_rows(rows):
    steps = rows // SUB
    r = lax.broadcasted_iota(jnp.int32, (rows + 2 * SUB, rows), 0)
    t = lax.broadcasted_iota(jnp.int32, (rows + 2 * SUB, rows), 1)
    return (t == (r & (SUB - 1)) * steps + (r >> 3) - 2).astype(F32).astype(BF16)


def scatter_rows(rows):
    steps = rows // SUB
    t = lax.broadcasted_iota(jnp.int32, (rows, rows), 0)
    r = lax.broadcasted_iota(jnp.int32, (rows, rows), 1)
    return (t == (r & (SUB - 1)) * steps + (r >> 3)).astype(F32).astype(BF16)


def featurize(perm, streams, taps, stream, at):
    x = jnp.dot(perm, streams[stream, :, at], preferred_element_type=F32)
    rows = x.shape[0] - 2 * SUB
    return (
        taps[0, pl.ds(stream, 1), at] * x[2 * SUB :]
        + taps[1, pl.ds(stream, 1), at] * x[SUB : SUB + rows]
        + taps[2, pl.ds(stream, 1), at] * x[:rows]
    )


def edge_terms(taps, stream, at, old, older):
    one = taps[1, pl.ds(stream, 1), at]
    two = taps[2, pl.ds(stream, 1), at]
    return one * old + two * older, two * old


def first_kernel(
    streams_hbm,
    taps_hbm,
    rates_hbm,
    residues_hbm,
    skip_hbm,
    base,
    gate,
    inner,
    reach,
    state,
    decay,
    streams,
    taps,
    rates,
    residues,
    skip,
    sig,
    heads,
    halo_out,
    halo_in,
    sbuf,
    abuf,
    tbuf,
    bbuf,
    hbuf,
    cbuf,
    load_sem,
    halo_sem,
    a_send,
    a_recv,
    b_send,
    b_recv,
    c_send,
    c_recv,
):
    rows, width = sig.shape
    steps = rows // SUB
    modes = rates.shape[0]
    tiles = width // LANES
    piece = width // GROUP
    me = lax.axis_index("ctx")
    count = lax.axis_size("ctx")
    outer = count // GROUP
    g = me // GROUP
    l = me - g * GROUP

    loads = [
        pltpu.make_async_copy(streams_hbm.at[1], streams.at[1], load_sem.at[0]),
        pltpu.make_async_copy(streams_hbm.at[2], streams.at[2], load_sem.at[1]),
        pltpu.make_async_copy(taps_hbm, taps, load_sem.at[2]),
        pltpu.make_async_copy(rates_hbm, rates, load_sem.at[3]),
        pltpu.make_async_copy(streams_hbm.at[0], streams.at[0], load_sem.at[4]),
        pltpu.make_async_copy(residues_hbm, residues, load_sem.at[5]),
        pltpu.make_async_copy(skip_hbm, skip, load_sem.at[6]),
    ]
    for load in loads:
        load.start()

    bar = pltpu.get_barrier_semaphore()
    for k in range(1, GROUP):
        pl.semaphore_signal(
            bar, inc=1, device_id={"ctx": g * GROUP + lax.rem(l + k, GROUP)}, device_id_type=MESH
        )
    for k in range(1, outer):
        pl.semaphore_signal(
            bar, inc=1, device_id={"ctx": lax.rem(g + k, outer) * GROUP + l}, device_id_type=MESH
        )
    pl.semaphore_signal(bar, inc=1, device_id={"ctx": lax.rem(me + 1, count)}, device_id_type=MESH)
    pl.semaphore_signal(
        bar, inc=1, device_id={"ctx": lax.rem(me + count - 1, count)}, device_id_type=MESH
    )

    perm = gather_rows(rows)
    for load in loads[:3]:
        load.wait()

    def signal_step(c, carry):
        at = lanes(c, 2 * LANES)
        one = featurize(perm, streams, taps, 1, at)
        two = featurize(perm, streams, taps, 2, at)
        sig[:, at] = one * two
        heads[0:1, at] = one[0:1]
        heads[1:2, at] = one[SUB : SUB + 1]
        heads[2:3, at] = two[0:1]
        heads[3:4, at] = two[SUB : SUB + 1]
        return carry

    lax.fori_loop(0, tiles // 2, signal_step, 0)

    loads[4].wait()
    for s in range(3):
        tail = streams[s, pl.ds(rows - 16, 16), :].astype(F32)
        halo_out[2 * s : 2 * s + 2, :] = tail[14:16]

    pl.semaphore_wait(bar, GROUP - 1 + outer - 1 + 2)
    halo = pltpu.make_async_remote_copy(
        src_ref=halo_out,
        dst_ref=halo_in,
        send_sem=halo_sem.at[0],
        recv_sem=halo_sem.at[1],
        device_id={"ctx": lax.rem(me + 1, count)},
        device_id_type=MESH,
    )

    @pl.when(me < count - 1)
    def _():
        halo.start()

    loads[3].wait()
    decay[...] = jnp.exp(-rates[...])

    sub_row = lax.broadcasted_iota(jnp.int32, (SUB, LANES), 0).astype(F32)
    to_end = (SUB - 1 - sub_row) * (-float(steps))

    def state_step(p, carry):
        for half in range(piece // LANES):
            at = lanes(p * (piece // LANES) + half)
            factor = [
                jnp.broadcast_to(decay[pl.ds(m, 1), at], (SUB, LANES)) for m in range(modes)
            ]
            held = [sig[0:SUB, at]] * modes
            for b in range(1, steps):
                x = sig[SUB * b : SUB * b + SUB, at]
                held = [h * f + x for h, f in zip(held, factor)]
            ends = []
            for m in range(modes):
                weight = jnp.exp(to_end * rates[pl.ds(m, 1), at])
                ends.append(jnp.sum(held[m] * weight, axis=0, keepdims=True))
            sbuf[p, :, half * LANES : half * LANES + LANES] = jnp.concatenate(ends, axis=0)
        return carry

    lax.fori_loop(0, GROUP, state_step, 0)

    @pl.when(me > 0)
    def _():
        halo.wait_recv()

    @pl.when(me == 0)
    def _():
        halo_in[...] = jnp.zeros_like(halo_in)

    def edge_step(p, carry):
        at = lanes(p, piece)
        one0, one1 = edge_terms(taps, 1, at, halo_in[3:4, at], halo_in[2:3, at])
        two0, two1 = edge_terms(taps, 2, at, halo_in[5:6, at], halo_in[4:5, at])
        new0 = (heads[0:1, at] + one0) * (heads[2:3, at] + two0)
        new1 = (heads[1:2, at] + one1) * (heads[3:4, at] + two1)
        add0 = new0 - sig[0:1, at]
        add1 = new1 - sig[SUB : SUB + 1, at]
        sig[0:1, at] = new0
        sig[SUB : SUB + 1, at] = new1
        rate = rates[:, at]
        sbuf[p] += jnp.exp(rate * (1.0 - rows)) * add0 + jnp.exp(rate * (2.0 - rows)) * add1
        return carry

    lax.fori_loop(0, GROUP, edge_step, 0)

    abuf[l] = sbuf[l]
    for k in range(1, GROUP):
        to = lax.rem(l + k, GROUP)
        pltpu.make_async_remote_copy(
            src_ref=sbuf.at[to],
            dst_ref=abuf.at[l],
            send_sem=a_send,
            recv_sem=a_recv,
            device_id={"ctx": g * GROUP + to},
            device_id_type=MESH,
        ).start()

    def gate_step(c, carry):
        at = lanes(c, 2 * LANES)
        gate[:, at] = featurize(perm, streams, taps, 0, at)
        zero0, zero1 = edge_terms(taps, 0, at, halo_in[1:2, at], halo_in[0:1, at])
        gate[0:1, at] += zero0
        gate[SUB : SUB + 1, at] += zero1
        return carry

    lax.fori_loop(0, tiles // 2, gate_step, 0)
    loads[5].wait()
    loads[6].wait()

    def own_step(c, carry):
        at = lanes(c)
        factor = [jnp.broadcast_to(decay[pl.ds(m, 1), at], (SUB, LANES)) for m in range(modes)]
        weight = [jnp.broadcast_to(residues[pl.ds(m, 1), at], (SUB, LANES)) for m in range(modes)]
        direct = jnp.broadcast_to(skip[0:1, at], (SUB, LANES))
        held = None
        for b in range(steps):
            x = sig[SUB * b : SUB * b + SUB, at]
            held = [x] * modes if b == 0 else [h * f + x for h, f in zip(held, factor)]
            total = direct * x
            for h, w in zip(held, weight):
                total = total + h * w
            base[SUB * b : SUB * b + SUB, at] = total
        for m in range(modes):
            rate = rates[pl.ds(m, 1), at]
            lead = weight[m] * factor[m]
            begin = jnp.where(sub_row < 1, 0.0, pltpu.roll(held[m], 1, 0))
            for reach_rows in (1, 2, 4):
                power = jnp.exp(rate * (-float(steps * reach_rows)))
                begin = begin + power * jnp.where(
                    sub_row < reach_rows, 0.0, pltpu.roll(begin, reach_rows, 0)
                )
            inner[c, m] = lead * begin
            reach[c, m] = lead * jnp.exp(sub_row * (rate * (-float(steps))))
        return carry

    lax.fori_loop(0, tiles // 4, own_step, 0)

    mine = lanes(l, piece)
    chunk_decay = jnp.exp(rates[:, mine] * (-float(rows)))
    group_decay = jnp.exp(rates[:, mine] * (-float(rows * GROUP)))
    others = pl.ds(0, GROUP - 1)
    pltpu.make_async_copy(sbuf.at[others], abuf.at[others], a_recv).wait()
    total = abuf[0]
    for k in range(1, GROUP):
        total = total * chunk_decay + abuf[k]
    tbuf[...] = total

    def group_copy(k):
        return pltpu.make_async_remote_copy(
            src_ref=tbuf,
            dst_ref=bbuf.at[g],
            send_sem=b_send.at[k],
            recv_sem=b_recv.at[g],
            device_id={"ctx": lax.rem(g + k, outer) * GROUP + l},
            device_id_type=MESH,
        )

    for k in range(1, outer):

        @pl.when(g + k < outer)
        def _():
            group_copy(k).start()

    lax.fori_loop(tiles // 4, 3 * tiles // 4, own_step, 0)

    hbuf[0] = jnp.zeros_like(total)
    for k in range(outer - 1):

        @pl.when(k < g)
        def _():
            pltpu.make_async_copy(tbuf, bbuf.at[k], b_recv.at[k]).wait()
            hbuf[0] = hbuf[0] * group_decay + bbuf[k]

    held = hbuf[0]
    for k in range(1, GROUP):
        held = held * chunk_decay + abuf[k - 1]
        hbuf[k] = held

    cbuf[l] = hbuf[l]
    for k in range(1, GROUP):
        to = lax.rem(l + k, GROUP)
        pltpu.make_async_remote_copy(
            src_ref=hbuf.at[to],
            dst_ref=cbuf.at[l],
            send_sem=c_send,
            recv_sem=c_recv,
            device_id={"ctx": g * GROUP + to},
            device_id_type=MESH,
        ).start()

    lax.fori_loop(3 * tiles // 4, tiles, own_step, 0)

    @pl.when(me < count - 1)
    def _():
        halo.wait_send()

    pltpu.make_async_copy(sbuf.at[others], abuf.at[others], a_send).wait()
    for k in range(1, outer):

        @pl.when(g + k < outer)
        def _():
            group_copy(k).wait_send()

    pltpu.make_async_copy(hbuf.at[others], cbuf.at[others], c_recv).wait()
    state[...] = cbuf[...]
    pltpu.make_async_copy(hbuf.at[others], cbuf.at[others], c_send).wait()


def second_kernel(base, gate, inner, reach, state, decay, out_hbm, out, out_sem):
    rows, width = out.shape
    steps = rows // SUB
    modes = decay.shape[0]
    tiles = width // LANES
    piece = width // GROUP
    parts = 4
    back = scatter_rows(rows)

    def tile_step(p, carry):
        for half in range(piece // LANES):
            c = p * (piece // LANES) + half
            at = lanes(c)
            factor = [
                jnp.broadcast_to(decay[pl.ds(m, 1), at], (SUB, LANES)) for m in range(modes)
            ]
            term = [
                inner[c, m]
                + reach[c, m] * state[p, pl.ds(m, 1), half * LANES : half * LANES + LANES]
                for m in range(modes)
            ]
            mixed = []
            for b in range(steps):
                total = base[SUB * b : SUB * b + SUB, at]
                for h in term:
                    total = total + h
                mixed.append((gate[SUB * b : SUB * b + SUB, at] * total).astype(F32))
                if b < steps - 1:
                    term = [h * f for h, f in zip(term, factor)]
            mixed = jnp.concatenate(mixed, axis=0).astype(BF16)
            out[:, at] = jnp.dot(back, mixed, preferred_element_type=F32).astype(BF16)
        return carry

    copies = []
    for q in range(parts):
        lax.fori_loop(q * GROUP // parts, (q + 1) * GROUP // parts, tile_step, 0)
        at = pl.ds(q * width // parts, width // parts)
        copies.append(pltpu.make_async_copy(out.at[:, at], out_hbm.at[:, at], out_sem.at[q]))
        copies[-1].start()
    for copy in copies:
        copy.wait()


def local(streams, short_filter, rates, residues, skip):
    _, rows, width = streams.shape
    modes = rates.shape[0]
    tiles = width // LANES
    piece = width // GROUP
    outer = lax.axis_size("ctx") // GROUP
    steps = rows // SUB
    any_spec = pl.BlockSpec(memory_space=pl.ANY)
    hbm_spec = pl.BlockSpec(memory_space=pltpu.HBM)
    vmem_spec = pl.BlockSpec(memory_space=pltpu.VMEM)
    pieces = pltpu.VMEM((GROUP, modes, piece), F32)
    parts = pl.pallas_call(
        first_kernel,
        out_shape=[
            pltpu.VMEM((rows, width), F32),
            pltpu.VMEM((rows, width), F32),
            pltpu.VMEM((tiles, modes, SUB, LANES), F32),
            pltpu.VMEM((tiles, modes, SUB, LANES), F32),
            pltpu.VMEM((GROUP, modes, piece), F32),
            pltpu.VMEM((modes, width), F32),
        ],
        in_specs=[hbm_spec] * 5,
        out_specs=[vmem_spec] * 6,
        scratch_shapes=[
            pltpu.VMEM(streams.shape, BF16),
            pltpu.VMEM(short_filter.shape, F32),
            pltpu.VMEM(rates.shape, F32),
            pltpu.VMEM(rates.shape, F32),
            pltpu.VMEM((1, width), F32),
            pltpu.VMEM((rows, width), F32),
            pltpu.VMEM((4, width), F32),
            pltpu.VMEM((8, width), F32),
            pltpu.VMEM((8, width), F32),
            pieces,
            pieces,
            pltpu.VMEM((modes, piece), F32),
            pltpu.VMEM((outer, modes, piece), F32),
            pieces,
            pieces,
            pltpu.SemaphoreType.DMA((7,)),
            pltpu.SemaphoreType.DMA((2,)),
            pltpu.SemaphoreType.DMA,
            pltpu.SemaphoreType.DMA,
            pltpu.SemaphoreType.DMA((outer,)),
            pltpu.SemaphoreType.DMA((outer,)),
            pltpu.SemaphoreType.DMA,
            pltpu.SemaphoreType.DMA,
        ],
        compiler_params=pltpu.CompilerParams(
            collective_id=0, has_side_effects=True, vmem_limit_bytes=24 * 1024 * 1024
        ),
        name="chunk_state",
    )(streams, short_filter, rates, residues, skip[None, :])
    return pl.pallas_call(
        second_kernel,
        out_shape=jax.ShapeDtypeStruct((rows, width), BF16),
        in_specs=[vmem_spec] * 6,
        out_specs=any_spec,
        scratch_shapes=[pltpu.VMEM((rows, width), BF16), pltpu.SemaphoreType.DMA((4,))],
        compiler_params=pltpu.CompilerParams(vmem_limit_bytes=24 * 1024 * 1024),
        name="mix",
    )(*parts)


def solution(mesh):
    placed = (
        P(None, "ctx", "chan"),
        P(None, None, "chan"),
        P(None, "chan"),
        P(None, "chan"),
        P("chan"),
    )
    return jax.shard_map(
        local, mesh=mesh, in_specs=placed, out_specs=P("ctx", "chan"), check_vma=False
    )
```

```python
import jax
import jax.numpy as jnp
from jax import lax
from jax.experimental import pallas as pl
from jax.experimental.pallas import tpu as pltpu
from jax.sharding import PartitionSpec as P

MESH = pl.DeviceIdType.MESH
LANES = 128
SUB = 8
GROUP = 8
CHIPS = GROUP // 2
F32 = jnp.float32
BF16 = jnp.bfloat16


def lanes(index, width=LANES):
    return pl.ds(pl.multiple_of(index * width, width), width)


def gather_rows(rows):
    steps = rows // SUB
    r = lax.broadcasted_iota(jnp.int32, (rows + 3 * SUB, rows), 0)
    t = lax.broadcasted_iota(jnp.int32, (rows + 3 * SUB, rows), 1)
    body = (r & (SUB - 1)) * steps + (r >> 3) - 2
    edge = (r & 3) + jnp.where((r & 3) < 2, 0, rows - 4)
    return (t == jnp.where(r < rows + 2 * SUB, body, edge)).astype(F32).astype(BF16)


def scatter_rows(rows):
    steps = rows // SUB
    t = lax.broadcasted_iota(jnp.int32, (rows, rows), 0)
    r = lax.broadcasted_iota(jnp.int32, (rows, rows), 1)
    return (t == (r & (SUB - 1)) * steps + (r >> 3)).astype(F32).astype(BF16)


def featurize(perm, streams, taps, stream, at):
    x = jnp.dot(perm, streams[stream, :, at], preferred_element_type=F32)
    rows = x.shape[0] - 3 * SUB
    features = (
        taps[0, pl.ds(stream, 1), at] * x[2 * SUB : 2 * SUB + rows]
        + taps[1, pl.ds(stream, 1), at] * x[SUB : SUB + rows]
        + taps[2, pl.ds(stream, 1), at] * x[:rows]
    )
    return features, x[2 * SUB + rows :]


def edge_features(weights, own, before):
    row = lax.broadcasted_iota(jnp.int32, own.shape, 0)
    one_back = jnp.where((row & 1) == 0, pltpu.roll(before, 5, 0), pltpu.roll(own, 1, 0))
    return weights[0] * own + weights[1] * one_back + weights[2] * pltpu.roll(before, 6, 0)


def edge_signal(weights, own, before):
    features = edge_features(weights, own, before)
    return features * pltpu.roll(features, 4, 0)


def edge_weights(taps, at):
    row = lax.broadcasted_iota(jnp.int32, (SUB, LANES), 0)
    return [jnp.where(row < 4, taps[j, 1:2, at], taps[j, 2:3, at]) for j in range(3)]


def kernel(
    streams_hbm,
    taps_hbm,
    rates_hbm,
    residues_hbm,
    skip_hbm,
    out,
    streams,
    taps,
    rates,
    residues,
    skip,
    decay,
    sig,
    gate,
    base,
    inner,
    reach,
    edges_out,
    edges_in,
    gate_edges_out,
    gate_edges_in,
    sbuf,
    abuf,
    full,
    tbuf,
    bbuf,
    hbuf,
    cbuf,
    load_sem,
    piece_sem,
    halo_sem,
    a_send,
    a_recv,
    b_send,
    b_recv,
    c_send,
    c_recv,
):
    rows, width = sig.shape
    steps = rows // SUB
    modes = rates.shape[0]
    tiles = width // LANES
    piece = width // GROUP
    halves = piece // LANES
    me = lax.axis_index("ctx")
    count = lax.axis_size("ctx")
    outer = count // GROUP
    g = me // GROUP
    l = me - g * GROUP
    chip = l // 2
    core = l - chip * 2

    def member(k):
        pair = k // 2
        hop = 2 - pair + 3 * (pair // 2) - 2 * (pair // 3)
        return 2 * lax.rem(chip + hop, CHIPS) + lax.rem(core + 1 + k, 2)

    taps_load = pltpu.make_async_copy(taps_hbm, taps, load_sem.at[0])
    rates_load = pltpu.make_async_copy(rates_hbm, rates, load_sem.at[1])
    late_loads = [
        pltpu.make_async_copy(streams_hbm.at[0], streams.at[0], load_sem.at[2]),
        pltpu.make_async_copy(residues_hbm, residues, load_sem.at[3]),
        pltpu.make_async_copy(skip_hbm, skip, load_sem.at[4]),
    ]

    def piece_load(k):
        at = lanes(member(k), piece)
        return pltpu.make_async_copy(
            streams_hbm.at[pl.ds(1, 2), :, at], streams.at[pl.ds(1, 2), :, at], piece_sem.at[k]
        )

    taps_load.start()
    piece_load(0).start()
    rates_load.start()

    bar = pltpu.get_barrier_semaphore()

    def greet(ctx):
        pl.semaphore_signal(bar, inc=1, device_id={"ctx": ctx}, device_id_type=MESH)

    for k in range(1, outer):
        greet(lax.rem(g + k, outer) * GROUP + l)
    for k in range(1, GROUP):
        greet(g * GROUP + lax.rem(l + k, GROUP))
    greet(lax.rem(me + 1, count))
    greet(lax.rem(me + count - 1, count))

    for k in range(1, GROUP):
        piece_load(k).start()
    for load in late_loads:
        load.start()

    perm = gather_rows(rows)
    sub_row = lax.broadcasted_iota(jnp.int32, (SUB, LANES), 0)
    sub_pos = sub_row.astype(F32) * float(steps)
    to_end = sub_pos - float(steps * (SUB - 1))

    def signal_of(k):
        p = member(k)
        at = lanes(p, piece)
        piece_load(k).wait()
        one, one_edge = featurize(perm, streams, taps, 1, at)
        two, two_edge = featurize(perm, streams, taps, 2, at)
        row = lax.broadcasted_iota(jnp.int32, (rows, piece), 0)
        sig[:, at] = jnp.where((row == 0) | (row == SUB), 0.0, one * two)
        edge_row = lax.broadcasted_iota(jnp.int32, (SUB, piece), 0)
        edges = jnp.where(edge_row < 4, one_edge, two_edge)
        edges = jnp.concatenate(
            [edges[:, h * LANES : h * LANES + LANES] for h in range(halves)], axis=0
        ).astype(BF16)
        edges_out[p] = edges
        sbuf[p, halves * modes :, :] = edges

    def state_of(k):
        p = member(k)
        for half in range(halves):
            at = lanes(p * halves + half)
            factor = [
                jnp.broadcast_to(decay[pl.ds(m, 1), at], (SUB, LANES)) for m in range(modes)
            ]
            held = [sig[0:SUB, at]] * modes
            for b in range(1, steps):
                x = sig[SUB * b : SUB * b + SUB, at]
                held = [h * f + x for h, f in zip(held, factor)]
            ends = []
            for m in range(modes):
                weight = jnp.exp(to_end * rates[pl.ds(m, 1), at])
                ends.append(jnp.sum(held[m] * weight, axis=0, keepdims=True))
            sbuf[p, half * modes : half * modes + modes, :] = jnp.concatenate(
                ends, axis=0
            ).astype(BF16)

    def first_send(k):
        to = member(k)
        return pltpu.make_async_remote_copy(
            src_ref=sbuf.at[to],
            dst_ref=abuf.at[l],
            send_sem=a_send,
            recv_sem=a_recv,
            device_id={"ctx": g * GROUP + to},
            device_id_type=MESH,
        )

    def halo_send(source, target, which):
        return pltpu.make_async_remote_copy(
            src_ref=source,
            dst_ref=target,
            send_sem=halo_sem.at[2 * which],
            recv_sem=halo_sem.at[2 * which + 1],
            device_id={"ctx": lax.rem(me + 1, count)},
            device_id_type=MESH,
        )

    taps_load.wait()
    signal_of(0)
    rates_load.wait()
    decay[...] = jnp.exp(-rates[...])

    def early_step(k, carry):
        state_of(k)
        signal_of(k + 1)
        return carry

    lax.fori_loop(0, GROUP - 2, early_step, 0)
    pl.semaphore_wait(bar, GROUP - 1 + outer - 1 + 2)

    def first_send_step(k, carry):
        first_send(k).start()
        return carry

    lax.fori_loop(0, GROUP - 2, first_send_step, 0)
    state_of(GROUP - 2)
    first_send(GROUP - 2).start()
    signal_of(GROUP - 1)
    halo = halo_send(edges_out, edges_in, 0)

    @pl.when(me < count - 1)
    def _():
        halo.start()

    state_of(GROUP - 1)
    abuf[l] = sbuf[l]

    for load in late_loads:
        load.wait()

    def gate_step(p, carry):
        at = lanes(p, piece)
        features, edges = featurize(perm, streams, taps, 0, at)
        gate[:, at] = features
        gate_edges_out[p] = jnp.concatenate(
            [edges[:, h * LANES : h * LANES + LANES] for h in range(halves)], axis=0
        ).astype(BF16)
        return carry

    lax.fori_loop(0, GROUP, gate_step, 0)
    gate_halo = halo_send(gate_edges_out, gate_edges_in, 1)

    @pl.when(me < count - 1)
    def _():
        gate_halo.start()

    def reach_step(c, carry):
        at = lanes(c)
        for m in range(modes):
            rate = rates[pl.ds(m, 1), at]
            lead = residues[pl.ds(m, 1), at] * decay[pl.ds(m, 1), at]
            reach[c, m] = lead * jnp.exp(-sub_pos * rate)
        return carry

    lax.fori_loop(0, tiles, reach_step, 0)

    for k in range(1, outer):

        @pl.when(k > g)
        def _():
            bbuf[k - 1] = jnp.zeros(bbuf.shape[1:], BF16)

    mine = [lanes(l * halves + half) for half in range(halves)]
    my_rates = [rates[:, at] for at in mine]
    my_weights = [edge_weights(taps, at) for at in mine]

    def power(n):
        return [jnp.exp(rate * (-float(n))) for rate in my_rates]

    def unpack(message):
        value = message.astype(F32)
        body = [value[h * modes : h * modes + modes] for h in range(halves)]
        edge = value[halves * modes :]
        return body, [edge[h * SUB : h * SUB + SUB] for h in range(halves)]

    def with_edge(body, first, second, own, before):
        done = []
        for h in range(halves):
            s = edge_signal(my_weights[h], own[h], before[h])
            done.append(body[h] + first[h] * s[0:1] + second[h] * s[1:2])
        return done

    chunk_decay = power(rows)
    to_first = power(rows - 1)
    to_second = power(rows - 2)
    others = pl.ds(0, GROUP - 1)
    pltpu.make_async_copy(sbuf.at[others], abuf.at[others], a_recv).wait()
    total, first_edge = unpack(abuf[0])
    first_body = total
    before = first_edge
    for k in range(1, GROUP):
        body, edge = unpack(abuf[k])
        body = with_edge(body, to_first, to_second, edge, before)
        for h in range(halves):
            full[k, h * modes : h * modes + modes, :] = body[h]
        total = [t * d + b for t, d, b in zip(total, chunk_decay, body)]
        before = edge
    group_edge = [jnp.where((sub_row & 3) < 2, a, b) for a, b in zip(first_edge, before)]
    tbuf[...] = jnp.concatenate(total + group_edge, axis=0).astype(BF16)

    def group_copy(k):
        return pltpu.make_async_remote_copy(
            src_ref=tbuf,
            dst_ref=bbuf.at[k - 1],
            send_sem=b_send.at[k - 1],
            recv_sem=b_recv.at[k - 1],
            device_id={"ctx": lax.rem(g + k, outer) * GROUP + l},
            device_id_type=MESH,
        )

    for k in (4, 5, 3, 6, 2, 7, 1):

        @pl.when(g + k < outer)
        def _():
            group_copy(k).start()

    @pl.when(me > 0)
    def _():
        halo.wait_recv()

    @pl.when(me == 0)
    def _():
        edges_in[...] = jnp.zeros_like(edges_in)

    def edge_step(p, carry):
        for h in range(halves):
            at = lanes(p * halves + h)
            part = slice(h * SUB, h * SUB + SUB)
            s = edge_signal(
                edge_weights(taps, at),
                edges_out[p].astype(F32)[part],
                edges_in[p].astype(F32)[part],
            )
            sig[0:1, at] = s[0:1]
            sig[SUB : SUB + 1, at] = s[1:2]
        return carry

    lax.fori_loop(0, GROUP, edge_step, 0)

    def own_step(c, carry):
        at = lanes(c)
        factor = [jnp.broadcast_to(decay[pl.ds(m, 1), at], (SUB, LANES)) for m in range(modes)]
        weight = [jnp.broadcast_to(residues[pl.ds(m, 1), at], (SUB, LANES)) for m in range(modes)]
        direct = jnp.broadcast_to(skip[0:1, at], (SUB, LANES))
        held = None
        for b in range(steps):
            x = sig[SUB * b : SUB * b + SUB, at]
            held = [x] * modes if b == 0 else [h * f + x for h, f in zip(held, factor)]
            terms = direct * x
            for h, w in zip(held, weight):
                terms = terms + h * w
            base[SUB * b : SUB * b + SUB, at] = terms
        for m in range(modes):
            rate = rates[pl.ds(m, 1), at]
            begin = jnp.where(sub_row < 1, 0.0, pltpu.roll(held[m], 1, 0))
            for back_rows in (1, 2, 4):
                begin = begin + jnp.exp(rate * (-float(steps * back_rows))) * jnp.where(
                    sub_row < back_rows, 0.0, pltpu.roll(begin, back_rows, 0)
                )
            inner[c, m] = weight[m] * factor[m] * begin
        return carry

    lax.fori_loop(0, tiles, own_step, 0)

    @pl.when(me > 0)
    def _():
        gate_halo.wait_recv()

    @pl.when(me == 0)
    def _():
        gate_edges_in[...] = jnp.zeros_like(gate_edges_in)

    def gate_edge_step(p, carry):
        for h in range(halves):
            at = lanes(p * halves + h)
            part = slice(h * SUB, h * SUB + SUB)
            f = edge_features(
                [taps[j, 0:1, at] for j in range(3)],
                gate_edges_out[p].astype(F32)[part],
                gate_edges_in[p].astype(F32)[part],
            )
            gate[0:1, at] = f[0:1]
            gate[SUB : SUB + 1, at] = f[1:2]
        return carry

    lax.fori_loop(0, GROUP, gate_edge_step, 0)

    group_decay = power(rows * GROUP)
    group_first = power(rows * GROUP - 1)
    group_second = power(rows * GROUP - 2)
    for k in range(1, outer):

        @pl.when(k <= g)
        def _():
            pltpu.make_async_copy(tbuf, bbuf.at[k - 1], b_recv.at[k - 1]).wait()

    held = [jnp.zeros((modes, LANES), F32)] * halves
    before = [jnp.zeros((SUB, LANES), F32)] * halves
    for k in range(outer - 1, 0, -1):
        body, edge = unpack(bbuf[k - 1])
        body = with_edge(body, group_first, group_second, edge, before)
        held = [h * d + b for h, d, b in zip(held, group_decay, body)]
        before = edge
    for k in range(GROUP):
        if k == 1:
            body = with_edge(first_body, to_first, to_second, first_edge, before)
        elif k > 1:
            body = [full[k - 1, h * modes : h * modes + modes, :] for h in range(halves)]
        if k > 0:
            held = [h * d + b for h, d, b in zip(held, chunk_decay, body)]
        hbuf[k] = jnp.concatenate(held, axis=0).astype(BF16)

    def last_send(k):
        to = member(k)
        return pltpu.make_async_remote_copy(
            src_ref=hbuf.at[to],
            dst_ref=cbuf.at[l],
            send_sem=c_send,
            recv_sem=c_recv.at[l],
            device_id={"ctx": g * GROUP + to},
            device_id_type=MESH,
        )

    def last_send_step(k, carry):
        last_send(k).start()
        return carry

    lax.fori_loop(0, GROUP - 1, last_send_step, 0)
    cbuf[l] = hbuf[l]
    back = scatter_rows(rows)

    def mix_of(p):
        mixed = []
        entering = cbuf[p].astype(F32)
        for half in range(halves):
            c = p * halves + half
            at = lanes(c)
            factor = [
                jnp.broadcast_to(decay[pl.ds(m, 1), at], (SUB, LANES)) for m in range(modes)
            ]
            term = [
                inner[c, m] + reach[c, m] * entering[half * modes + m : half * modes + m + 1]
                for m in range(modes)
            ]
            column = []
            for b in range(steps):
                terms = base[SUB * b : SUB * b + SUB, at]
                for h in term:
                    terms = terms + h
                column.append(gate[SUB * b : SUB * b + SUB, at] * terms)
                if b < steps - 1:
                    term = [h * f for h, f in zip(term, factor)]
            mixed.append(jnp.concatenate(column, axis=0).astype(BF16))
        mixed = jnp.concatenate(mixed, axis=1)
        out[:, lanes(p, piece)] = jnp.dot(back, mixed, preferred_element_type=F32).astype(BF16)

    mix_of(l)

    def mix_step(k, carry):
        p = member(GROUP - 2 - k)
        pltpu.make_async_copy(hbuf.at[p], cbuf.at[p], c_recv.at[p]).wait()
        mix_of(p)
        return carry

    lax.fori_loop(0, GROUP - 1, mix_step, 0)

    @pl.when(me < count - 1)
    def _():
        halo.wait_send()
        gate_halo.wait_send()

    pltpu.make_async_copy(sbuf.at[others], abuf.at[others], a_send).wait()
    pltpu.make_async_copy(hbuf.at[others], cbuf.at[others], c_send).wait()
    for k in range(1, outer):

        @pl.when(g + k < outer)
        def _():
            group_copy(k).wait_send()


def local(streams, short_filter, rates, residues, skip):
    _, rows, width = streams.shape
    modes = rates.shape[0]
    tiles = width // LANES
    halves = tiles // GROUP
    outer = lax.axis_size("ctx") // GROUP
    args = (streams, short_filter, rates, residues, skip[None, :])
    wide = pltpu.VMEM((rows, width), F32)
    per_mode = pltpu.VMEM((tiles, modes, SUB, LANES), F32)
    edges = pltpu.VMEM((GROUP, halves * SUB, LANES), BF16)
    body = halves * modes
    message = body + halves * SUB
    dma = pltpu.SemaphoreType.DMA
    return pl.pallas_call(
        kernel,
        out_shape=pltpu.VMEM((rows, width), BF16),
        in_specs=[pl.BlockSpec(memory_space=pltpu.HBM)] * len(args),
        out_specs=pl.BlockSpec(memory_space=pltpu.VMEM),
        scratch_shapes=[
            pltpu.VMEM(streams.shape, BF16),
            pltpu.VMEM(short_filter.shape, F32),
            pltpu.VMEM(rates.shape, F32),
            pltpu.VMEM(rates.shape, F32),
            pltpu.VMEM((1, width), F32),
            pltpu.VMEM(rates.shape, F32),
            wide,
            wide,
            wide,
            per_mode,
            per_mode,
            edges,
            edges,
            edges,
            edges,
            pltpu.VMEM((GROUP, message, LANES), BF16),
            pltpu.VMEM((GROUP, message, LANES), BF16),
            pltpu.VMEM((GROUP, body, LANES), F32),
            pltpu.VMEM((message, LANES), BF16),
            pltpu.VMEM((outer - 1, message, LANES), BF16),
            pltpu.VMEM((GROUP, body, LANES), BF16),
            pltpu.VMEM((GROUP, body, LANES), BF16),
            dma((5,)),
            dma((GROUP,)),
            dma((4,)),
            dma,
            dma,
            dma((outer - 1,)),
            dma((outer - 1,)),
            dma,
            dma((GROUP,)),
        ],
        compiler_params=pltpu.CompilerParams(
            collective_id=0, has_side_effects=True, vmem_limit_bytes=24 * 1024 * 1024
        ),
        name="mixer",
    )(*(pltpu.with_memory_space_constraint(a, pltpu.HBM) for a in args))


def solution(mesh):
    placed = (
        P(None, "ctx", "chan"),
        P(None, None, "chan"),
        P(None, "chan"),
        P(None, "chan"),
        P("chan"),
    )
    return jax.shard_map(
        local, mesh=mesh, in_specs=placed, out_specs=P("ctx", "chan"), check_vma=False
    )
```

```python
import jax
import jax.numpy as jnp
from jax import lax
from jax.experimental import pallas as pl
from jax.experimental.pallas import tpu as pltpu
from jax.sharding import PartitionSpec as P

MESH = pl.DeviceIdType.MESH
LANES = 128
ANSWER_AT = 1
LATE_TILES = 4
SUB = 8
GROUP = 8
CHIPS = GROUP // 2
F32 = jnp.float32
BF16 = jnp.bfloat16


def lanes(index, width=LANES):
    return pl.ds(pl.multiple_of(index * width, width), width)


def gather_rows(rows):
    steps = rows // SUB
    r = lax.broadcasted_iota(jnp.int32, (rows + 3 * SUB, rows), 0)
    t = lax.broadcasted_iota(jnp.int32, (rows + 3 * SUB, rows), 1)
    body = (r & (SUB - 1)) * steps + (r >> 3) - 2
    edge = (r & 3) + jnp.where((r & 3) < 2, 0, rows - 4)
    return (t == jnp.where(r < rows + 2 * SUB, body, edge)).astype(F32).astype(BF16)


def scatter_rows(rows):
    steps = rows // SUB
    t = lax.broadcasted_iota(jnp.int32, (rows, rows), 0)
    r = lax.broadcasted_iota(jnp.int32, (rows, rows), 1)
    return (t == (r & (SUB - 1)) * steps + (r >> 3)).astype(F32).astype(BF16)


def featurize(perm, streams, taps, stream, at):
    x = jnp.dot(perm, streams[stream, :, at], preferred_element_type=F32)
    rows = x.shape[0] - 3 * SUB
    features = (
        taps[0, pl.ds(stream, 1), at] * x[2 * SUB : 2 * SUB + rows]
        + taps[1, pl.ds(stream, 1), at] * x[SUB : SUB + rows]
        + taps[2, pl.ds(stream, 1), at] * x[:rows]
    )
    return features, x[2 * SUB + rows :]


def edge_features(weights, own, before):
    row = lax.broadcasted_iota(jnp.int32, own.shape, 0)
    one_back = jnp.where((row & 1) == 0, pltpu.roll(before, 5, 0), pltpu.roll(own, 1, 0))
    return weights[0] * own + weights[1] * one_back + weights[2] * pltpu.roll(before, 6, 0)


def edge_signal(weights, own, before):
    features = edge_features(weights, own, before)
    return features * pltpu.roll(features, 4, 0)


def edge_weights(taps, at):
    row = lax.broadcasted_iota(jnp.int32, (SUB, LANES), 0)
    return [jnp.where(row < 4, taps[j, 1:2, at], taps[j, 2:3, at]) for j in range(3)]


def kernel(
    streams_hbm,
    taps_hbm,
    rates_hbm,
    residues_hbm,
    skip_hbm,
    out,
    streams,
    taps,
    rates,
    residues,
    skip,
    decay,
    sig,
    gate,
    base,
    inner,
    reach,
    edges_out,
    edges_in,
    gate_edges_out,
    gate_edges_in,
    sbuf,
    abuf,
    full,
    extra,
    tbuf,
    bbuf,
    hbuf,
    cbuf,
    entering,
    ready_a,
    ready_b,
    load_sem,
    piece_sem,
    halo_sem,
    mates_in,
    groups_in,
    next_in,
    a_send,
    a_recv,
    b_send,
    b_recv,
    c_send,
    c_recv,
):
    rows, width = sig.shape
    steps = rows // SUB
    modes = rates.shape[0]
    tiles = width // LANES
    piece = width // GROUP
    halves = piece // LANES
    me = lax.axis_index("ctx")
    count = lax.axis_size("ctx")
    outer = count // GROUP
    half = outer // 2
    g = me // GROUP
    l = me - g * GROUP
    chip = l // 2
    core = l - chip * 2

    def earlier_mates(at):
        c = at // 2
        return 2 * (c + c // 2 - 2 * (c // 3)) + 1 - (at - 2 * c)

    def member(k):
        pair = k // 2
        hop = 2 - pair + 3 * (pair // 2) - 2 * (pair // 3)
        return 2 * lax.rem(chip + hop, CHIPS) + lax.rem(core + 1 + k, 2)

    taps_load = pltpu.make_async_copy(taps_hbm, taps, load_sem.at[0])
    rates_load = pltpu.make_async_copy(rates_hbm, rates, load_sem.at[1])
    late_loads = [
        pltpu.make_async_copy(streams_hbm.at[0], streams.at[0], load_sem.at[2]),
        pltpu.make_async_copy(residues_hbm, residues, load_sem.at[3]),
        pltpu.make_async_copy(skip_hbm, skip, load_sem.at[4]),
    ]

    def piece_load(k):
        at = lanes(member(k), piece)
        return pltpu.make_async_copy(
            streams_hbm.at[pl.ds(1, 2), :, at], streams.at[pl.ds(1, 2), :, at], piece_sem.at[k]
        )

    taps_load.start()
    piece_load(0).start()
    rates_load.start()

    bar = pltpu.get_barrier_semaphore()

    def greet(ctx):
        pl.semaphore_signal(bar, inc=1, device_id={"ctx": ctx}, device_id_type=MESH)

    def along(other):
        return other * GROUP + l

    for k in range(1, GROUP):
        mate = lax.rem(l + k, GROUP)

        @pl.when(earlier_mates(mate) > earlier_mates(l))
        def _():
            greet(g * GROUP + mate)

    first_half = g < half
    for k in range(1, outer):

        @pl.when((g + k < outer) & (first_half | (k == 1)))
        def _():
            greet(along(g + k))

    @pl.when(g > half)
    def _():
        greet(along(g - 1))

    greetings = (
        earlier_mates(l)
        + jnp.minimum(g, half)
        + jnp.where(g > half, 1, 0)
        + jnp.where((g >= half) & (g < outer - 1), 1, 0)
    )

    for k in range(1, GROUP):
        piece_load(k).start()
    for load in late_loads:
        load.start()

    perm = gather_rows(rows)
    sub_row = lax.broadcasted_iota(jnp.int32, (SUB, LANES), 0)
    sub_pos = sub_row.astype(F32) * float(steps)
    to_end = sub_pos - float(steps * (SUB - 1))

    def signal_of(k):
        p = member(k)
        at = lanes(p, piece)
        piece_load(k).wait()
        one, one_edge = featurize(perm, streams, taps, 1, at)
        two, two_edge = featurize(perm, streams, taps, 2, at)
        row = lax.broadcasted_iota(jnp.int32, (rows, piece), 0)
        sig[:, at] = jnp.where((row == 0) | (row == SUB), 0.0, one * two)
        edge_row = lax.broadcasted_iota(jnp.int32, (SUB, piece), 0)
        edges = jnp.where(edge_row < 4, one_edge, two_edge)
        edges = jnp.concatenate(
            [edges[:, h * LANES : h * LANES + LANES] for h in range(halves)], axis=0
        ).astype(BF16)
        edges_out[p] = edges
        sbuf[p, halves * modes :, :] = edges

    def state_of(k):
        p = member(k)
        for half in range(halves):
            at = lanes(p * halves + half)
            factor = [
                jnp.broadcast_to(decay[pl.ds(m, 1), at], (SUB, LANES)) for m in range(modes)
            ]
            held = [sig[0:SUB, at]] * modes
            for b in range(1, steps):
                x = sig[SUB * b : SUB * b + SUB, at]
                held = [h * f + x for h, f in zip(held, factor)]
            ends = []
            for m in range(modes):
                weight = jnp.exp(to_end * rates[pl.ds(m, 1), at])
                ends.append(jnp.sum(held[m] * weight, axis=0, keepdims=True))
            sbuf[p, half * modes : half * modes + modes, :] = jnp.concatenate(
                ends, axis=0
            ).astype(BF16)

    def first_send(k):
        to = member(k)
        return pltpu.make_async_remote_copy(
            src_ref=sbuf.at[to],
            dst_ref=abuf.at[l],
            send_sem=a_send,
            recv_sem=a_recv,
            device_id={"ctx": g * GROUP + to},
            device_id_type=MESH,
        )

    def halo_send(source, target, which):
        return pltpu.make_async_remote_copy(
            src_ref=source,
            dst_ref=target,
            send_sem=halo_sem.at[2 * which],
            recv_sem=halo_sem.at[2 * which + 1],
            device_id={"ctx": lax.rem(me + 1, count)},
            device_id_type=MESH,
        )

    taps_load.wait()
    signal_of(0)
    rates_load.wait()
    decay[...] = jnp.exp(-rates[...])

    def early_step(k, carry):
        state_of(k)
        signal_of(k + 1)
        return carry

    lax.fori_loop(0, ANSWER_AT, early_step, 0)

    @pl.when(greetings > 0)
    def _():
        pl.semaphore_wait(bar, greetings)

    for k in range(1, GROUP):
        mate = lax.rem(l + k, GROUP)

        @pl.when(earlier_mates(mate) < earlier_mates(l))
        def _():
            pl.semaphore_signal(
                mates_in, inc=1, device_id={"ctx": g * GROUP + mate}, device_id_type=MESH
            )

    def tell_group(other, k):
        pl.semaphore_signal(
            groups_in.at[k - 1], inc=1, device_id={"ctx": along(other)}, device_id_type=MESH
        )

    for k in range(1, outer):

        @pl.when((k <= g) & (g - k < half))
        def _():
            tell_group(g - k, k)

    @pl.when((g > half) & (g < outer - 1))
    def _():
        tell_group(g - 1, 2)

    lax.fori_loop(ANSWER_AT, GROUP - 2, early_step, 0)
    answers = GROUP - 1 - earlier_mates(l)

    @pl.when(answers > 0)
    def _():
        pl.semaphore_wait(mates_in, answers)


    def first_send_step(k, carry):
        first_send(k).start()
        return carry

    lax.fori_loop(0, GROUP - 2, first_send_step, 0)
    state_of(GROUP - 2)
    first_send(GROUP - 2).start()
    signal_of(GROUP - 1)
    state_of(GROUP - 1)
    abuf[l] = sbuf[l]

    @pl.when(g == half + 1)
    def _():
        pl.semaphore_wait(groups_in.at[1], 1)
        tell_group(half, 3)


    for load in late_loads:
        load.wait()

    def gate_step(p, carry):
        at = lanes(p, piece)
        features, edges = featurize(perm, streams, taps, 0, at)
        gate[:, at] = features
        gate_edges_out[p] = jnp.concatenate(
            [edges[:, h * LANES : h * LANES + LANES] for h in range(halves)], axis=0
        ).astype(BF16)
        return carry

    lax.fori_loop(0, GROUP, gate_step, 0)
    halo = halo_send(edges_out, edges_in, 0)
    gate_halo = halo_send(gate_edges_out, gate_edges_in, 1)

    @pl.when(l < GROUP - 1)
    def _():
        halo.start()
        gate_halo.start()

    @pl.when((l == 0) & (g < outer - 1))
    def _():
        @pl.when(first_half)
        def _():
            pl.semaphore_wait(groups_in.at[0], 1)

        pl.semaphore_signal(
            next_in, inc=1, device_id={"ctx": me + GROUP - 1}, device_id_type=MESH
        )

    def reach_step(c, carry):
        at = lanes(c)
        for m in range(modes):
            rate = rates[pl.ds(m, 1), at]
            lead = residues[pl.ds(m, 1), at] * decay[pl.ds(m, 1), at]
            reach[c, m] = lead * jnp.exp(-sub_pos * rate)
        return carry

    lax.fori_loop(0, tiles, reach_step, 0)

    def own_step(c, carry):
        at = lanes(c)
        factor = [jnp.broadcast_to(decay[pl.ds(m, 1), at], (SUB, LANES)) for m in range(modes)]
        weight = [jnp.broadcast_to(residues[pl.ds(m, 1), at], (SUB, LANES)) for m in range(modes)]
        direct = jnp.broadcast_to(skip[0:1, at], (SUB, LANES))
        held = None
        for b in range(steps):
            x = sig[SUB * b : SUB * b + SUB, at]
            held = [x] * modes if b == 0 else [h * f + x for h, f in zip(held, factor)]
            terms = direct * x
            for h, w in zip(held, weight):
                terms = terms + h * w
            base[SUB * b : SUB * b + SUB, at] = terms
        for m in range(modes):
            rate = rates[pl.ds(m, 1), at]
            begin = jnp.where(sub_row < 1, 0.0, pltpu.roll(held[m], 1, 0))
            for back_rows in (1, 2, 4):
                begin = begin + jnp.exp(rate * (-float(steps * back_rows))) * jnp.where(
                    sub_row < back_rows, 0.0, pltpu.roll(begin, back_rows, 0)
                )
            inner[c, m] = weight[m] * factor[m] * begin
        return carry

    early_tiles = tiles - LATE_TILES * (earlier_mates(l) // 2)
    lax.fori_loop(0, early_tiles, own_step, 0)

    @pl.when((l == GROUP - 1) & (g < outer - 1))
    def _():
        pl.semaphore_wait(next_in, 1)
        halo.start()
        gate_halo.start()

    for k in range(1, outer):

        @pl.when(k > g)
        def _():
            bbuf[k - 1] = jnp.zeros(bbuf.shape[1:], BF16)

    mine = [lanes(l * halves + half) for half in range(halves)]
    my_rates = [rates[:, at] for at in mine]
    my_weights = [edge_weights(taps, at) for at in mine]

    def power(n):
        return [jnp.exp(rate * (-float(n))) for rate in my_rates]

    def unpack(message):
        value = message.astype(F32)
        body = [value[h * modes : h * modes + modes] for h in range(halves)]
        edge = value[halves * modes :]
        return body, [edge[h * SUB : h * SUB + SUB] for h in range(halves)]

    def with_edge(body, first, second, own, before):
        done = []
        for h in range(halves):
            s = edge_signal(my_weights[h], own[h], before[h])
            done.append(body[h] + first[h] * s[0:1] + second[h] * s[1:2])
        return done

    chunk_decay = power(rows)
    to_first = power(rows - 1)
    to_second = power(rows - 2)
    others = pl.ds(0, GROUP - 1)
    pltpu.make_async_copy(sbuf.at[others], abuf.at[others], a_recv).wait()
    total, first_edge = unpack(abuf[0])
    first_body = total
    before = first_edge
    for k in range(1, GROUP):
        body, edge = unpack(abuf[k])
        body = with_edge(body, to_first, to_second, edge, before)
        for h in range(halves):
            full[k, h * modes : h * modes + modes, :] = body[h]
        total = [t * d + b for t, d, b in zip(total, chunk_decay, body)]
        before = edge
    group_edge = [jnp.where((sub_row & 3) < 2, a, b) for a, b in zip(first_edge, before)]
    tbuf[...] = jnp.concatenate(total + group_edge, axis=0).astype(BF16)

    def group_copy(k):
        return pltpu.make_async_remote_copy(
            src_ref=tbuf,
            dst_ref=bbuf.at[k - 1],
            send_sem=b_send.at[k - 1],
            recv_sem=b_recv.at[k - 1],
            device_id={"ctx": along(g + k)},
            device_id_type=MESH,
        )

    def group_send(k):
        @pl.when(g + k < outer)
        def _():
            waited = ((k == 1) & (l == 0)) | ((k == 2) & (g == half + 1))

            @pl.when((first_half | (k > 1)) & jnp.logical_not(waited))
            def _():
                pl.semaphore_wait(groups_in.at[k - 1], 1)

            group_copy(k).start()

    for k in range(1, outer):
        group_send(k)

    one_up = power(-1)
    two_up = power(-2)

    def boost(own, before):
        done = []
        for h in range(halves):
            s = edge_signal(my_weights[h], own[h], before[h])
            done.append(one_up[h] * s[0:1] + two_up[h] * s[1:2])
        return done

    before = first_edge
    for k in range(1, GROUP):
        edge = unpack(abuf[k])[1]
        extra[k] = jnp.concatenate(boost(edge, before), axis=0)
        before = edge

    group_decay = power(rows * GROUP)
    group_first = power(rows * GROUP - 1)
    group_second = power(rows * GROUP - 2)
    for k in range(1, outer):

        @pl.when(k <= g)
        def _():
            pltpu.make_async_copy(tbuf, bbuf.at[k - 1], b_recv.at[k - 1]).wait()

    held = [jnp.zeros((modes, LANES), F32)] * halves
    before = [jnp.zeros((SUB, LANES), F32)] * halves
    for k in range(outer - 1, 0, -1):
        body, edge = unpack(bbuf[k - 1])
        body = with_edge(body, group_first, group_second, edge, before)
        held = [h * d + b for h, d, b in zip(held, group_decay, body)]
        before = edge
    extra[0] = jnp.concatenate(boost(first_edge, before), axis=0)
    for k in range(GROUP):
        if k == 1:
            body = with_edge(first_body, to_first, to_second, first_edge, before)
        elif k > 1:
            body = [full[k - 1, h * modes : h * modes + modes, :] for h in range(halves)]
        if k > 0:
            held = [h * d + b for h, d, b in zip(held, chunk_decay, body)]
        hbuf[k] = (jnp.concatenate(held, axis=0) + extra[k]).astype(BF16)

    def last_send(k):
        to = member(k)
        return pltpu.make_async_remote_copy(
            src_ref=hbuf.at[to],
            dst_ref=cbuf.at[l],
            send_sem=c_send,
            recv_sem=c_recv.at[l],
            device_id={"ctx": g * GROUP + to},
            device_id_type=MESH,
        )

    def last_send_step(k, carry):
        last_send(k).start()
        return carry

    lax.fori_loop(0, GROUP - 1, last_send_step, 0)
    cbuf[l] = hbuf[l]
    back = scatter_rows(rows)
    lax.fori_loop(early_tiles, tiles, own_step, 0)

    @pl.when(me > 0)
    def _():
        halo.wait_recv()

    @pl.when(me == 0)
    def _():
        edges_in[...] = jnp.zeros_like(edges_in)

    def edge_step(p, carry):
        for h in range(halves):
            at = lanes(p * halves + h)
            part = slice(h * SUB, h * SUB + SUB)
            s = edge_signal(
                edge_weights(taps, at),
                edges_out[p].astype(F32)[part],
                edges_in[p].astype(F32)[part],
            )
            ahead = jnp.sum(residues[:, at] * jnp.exp(rates[:, at]), axis=0, keepdims=True)
            base[0:1, at] += skip[0:1, at] * s[0:1] - ahead * s[1:2]
            base[SUB : SUB + 1, at] += skip[0:1, at] * s[1:2]
        return carry

    lax.fori_loop(0, GROUP, edge_step, 0)

    @pl.when(me > 0)
    def _():
        gate_halo.wait_recv()

    @pl.when(me == 0)
    def _():
        gate_edges_in[...] = jnp.zeros_like(gate_edges_in)

    def gate_edge_step(p, carry):
        for h in range(halves):
            at = lanes(p * halves + h)
            part = slice(h * SUB, h * SUB + SUB)
            f = edge_features(
                [taps[j, 0:1, at] for j in range(3)],
                gate_edges_out[p].astype(F32)[part],
                gate_edges_in[p].astype(F32)[part],
            )
            gate[0:1, at] = f[0:1]
            gate[SUB : SUB + 1, at] = f[1:2]
        return carry

    lax.fori_loop(0, GROUP, gate_edge_step, 0)


    def mix_of(p, ready):
        entering[...] = cbuf[p].astype(F32)
        for half in range(halves):
            c = p * halves + half
            at = lanes(c)
            factor = [
                jnp.broadcast_to(decay[pl.ds(m, 1), at], (SUB, LANES)) for m in range(modes)
            ]
            term = [
                inner[c, m] + reach[c, m] * entering[pl.ds(half * modes + m, 1), :]
                for m in range(modes)
            ]
            column = []
            for b in range(steps):
                terms = base[SUB * b : SUB * b + SUB, at]
                for h in term:
                    terms = terms + h
                column.append(gate[SUB * b : SUB * b + SUB, at] * terms)
                if b < steps - 1:
                    term = [h * f for h, f in zip(term, factor)]
            ready[:, half * LANES : half * LANES + LANES] = jnp.concatenate(
                column, axis=0
            ).astype(BF16)

    def put_back(p, ready):
        out[:, lanes(p, piece)] = jnp.dot(
            back, ready[...], preferred_element_type=F32
        ).astype(BF16)

    def mix_next(k, ready, last_ready):
        p = member(k)
        pltpu.make_async_copy(hbuf.at[p], cbuf.at[p], c_recv.at[p]).wait()
        put_back(member(k + 1), last_ready)
        mix_of(p, ready)

    mix_of(l, ready_a)

    def mix_pair(j, carry):
        mix_next(GROUP - 2 - 2 * j, ready_b, ready_a)
        mix_next(GROUP - 3 - 2 * j, ready_a, ready_b)
        return carry

    lax.fori_loop(0, GROUP // 2 - 1, mix_pair, 0)
    mix_next(0, ready_b, ready_a)
    put_back(member(0), ready_b)

    @pl.when(me < count - 1)
    def _():
        halo.wait_send()
        gate_halo.wait_send()

    pltpu.make_async_copy(sbuf.at[others], abuf.at[others], a_send).wait()
    pltpu.make_async_copy(hbuf.at[others], cbuf.at[others], c_send).wait()
    for k in range(1, outer):

        @pl.when(g + k < outer)
        def _():
            group_copy(k).wait_send()


def local(streams, short_filter, rates, residues, skip):
    _, rows, width = streams.shape
    modes = rates.shape[0]
    tiles = width // LANES
    halves = tiles // GROUP
    outer = lax.axis_size("ctx") // GROUP
    args = (streams, short_filter, rates, residues, skip[None, :])
    wide = pltpu.VMEM((rows, width), F32)
    per_mode = pltpu.VMEM((tiles, modes, SUB, LANES), F32)
    edges = pltpu.VMEM((GROUP, halves * SUB, LANES), BF16)
    body = halves * modes
    message = body + halves * SUB
    dma = pltpu.SemaphoreType.DMA
    return pl.pallas_call(
        kernel,
        out_shape=pltpu.VMEM((rows, width), BF16),
        in_specs=[pl.BlockSpec(memory_space=pltpu.HBM)] * len(args),
        out_specs=pl.BlockSpec(memory_space=pltpu.VMEM),
        scratch_shapes=[
            pltpu.VMEM(streams.shape, BF16),
            pltpu.VMEM(short_filter.shape, F32),
            pltpu.VMEM(rates.shape, F32),
            pltpu.VMEM(rates.shape, F32),
            pltpu.VMEM((1, width), F32),
            pltpu.VMEM(rates.shape, F32),
            wide,
            wide,
            wide,
            per_mode,
            per_mode,
            edges,
            edges,
            edges,
            edges,
            pltpu.VMEM((GROUP, message, LANES), BF16),
            pltpu.VMEM((GROUP, message, LANES), BF16),
            pltpu.VMEM((GROUP, body, LANES), F32),
            pltpu.VMEM((GROUP, body, LANES), F32),
            pltpu.VMEM((message, LANES), BF16),
            pltpu.VMEM((outer - 1, message, LANES), BF16),
            pltpu.VMEM((GROUP, body, LANES), BF16),
            pltpu.VMEM((GROUP, body, LANES), BF16),
            pltpu.VMEM((body, LANES), F32),
            pltpu.VMEM((rows, halves * LANES), BF16),
            pltpu.VMEM((rows, halves * LANES), BF16),
            dma((5,)),
            dma((GROUP,)),
            dma((4,)),
            pltpu.SemaphoreType.REGULAR,
            pltpu.SemaphoreType.REGULAR((outer - 1,)),
            pltpu.SemaphoreType.REGULAR,
            dma,
            dma,
            dma((outer - 1,)),
            dma((outer - 1,)),
            dma,
            dma((GROUP,)),
        ],
        compiler_params=pltpu.CompilerParams(
            collective_id=0, has_side_effects=True, vmem_limit_bytes=24 * 1024 * 1024
        ),
        name="mixer",
    )(*(pltpu.with_memory_space_constraint(a, pltpu.HBM) for a in args))


def solution(mesh):
    placed = (
        P(None, "ctx", "chan"),
        P(None, None, "chan"),
        P(None, "chan"),
        P(None, "chan"),
        P("chan"),
    )
    return jax.shard_map(
        local, mesh=mesh, in_specs=placed, out_specs=P("ctx", "chan"), check_vma=False
    )
```

```python
import jax
import jax.numpy as jnp
from jax import lax
from jax.experimental import pallas as pl
from jax.experimental.pallas import tpu as pltpu
from jax.sharding import PartitionSpec as P

MESH = pl.DeviceIdType.MESH
LANES = 128
LAST_ANSWER_AT = 6
ANSWER_LESS = 2
EARLY_TILES = 10
EARLY_LESS = 3
MIDDLE_TILES = 4
FEW_MIDDLE = 0
SUB = 8
GROUP = 8
CHIPS = GROUP // 2
F32 = jnp.float32
BF16 = jnp.bfloat16


def lanes(index, width=LANES):
    return pl.ds(pl.multiple_of(index * width, width), width)


def gather_rows(rows):
    steps = rows // SUB
    r = lax.broadcasted_iota(jnp.int32, (rows + 3 * SUB, rows), 0)
    t = lax.broadcasted_iota(jnp.int32, (rows + 3 * SUB, rows), 1)
    body = (r & (SUB - 1)) * steps + (r >> 3) - 2
    edge = (r & 3) + jnp.where((r & 3) < 2, 0, rows - 4)
    return (t == jnp.where(r < rows + 2 * SUB, body, edge)).astype(F32).astype(BF16)


def scatter_rows(rows):
    steps = rows // SUB
    t = lax.broadcasted_iota(jnp.int32, (rows, rows), 0)
    r = lax.broadcasted_iota(jnp.int32, (rows, rows), 1)
    return (t == (r & (SUB - 1)) * steps + (r >> 3)).astype(F32).astype(BF16)


def featurize(perm, streams, taps, stream, at):
    x = jnp.dot(perm, streams[stream, :, at], preferred_element_type=F32)
    rows = x.shape[0] - 3 * SUB
    features = (
        taps[0, pl.ds(stream, 1), at] * x[2 * SUB : 2 * SUB + rows]
        + taps[1, pl.ds(stream, 1), at] * x[SUB : SUB + rows]
        + taps[2, pl.ds(stream, 1), at] * x[:rows]
    )
    return features, x[2 * SUB + rows :]


def edge_features(weights, own, before):
    row = lax.broadcasted_iota(jnp.int32, own.shape, 0)
    one_back = jnp.where((row & 1) == 0, pltpu.roll(before, 5, 0), pltpu.roll(own, 1, 0))
    return weights[0] * own + weights[1] * one_back + weights[2] * pltpu.roll(before, 6, 0)


def edge_signal(weights, own, before):
    features = edge_features(weights, own, before)
    return features * pltpu.roll(features, 4, 0)


def edge_weights(taps, at):
    row = lax.broadcasted_iota(jnp.int32, (SUB, LANES), 0)
    return [jnp.where(row < 4, taps[j, 1:2, at], taps[j, 2:3, at]) for j in range(3)]


def kernel(
    streams_hbm,
    taps_hbm,
    rates_hbm,
    residues_hbm,
    skip_hbm,
    out,
    streams,
    taps,
    rates,
    residues,
    skip,
    decay,
    sig,
    gate,
    base,
    inner,
    reach,
    edges_out,
    edges_in,
    gate_edges_out,
    gate_edges_in,
    sbuf,
    abuf,
    full,
    extra,
    tbuf,
    bbuf,
    hbuf,
    cbuf,
    entering,
    ready_a,
    ready_b,
    load_sem,
    piece_sem,
    halo_sem,
    groups_in,
    next_in,
    a_send,
    a_recv,
    b_send,
    b_recv,
    c_send,
    c_recv,
):
    rows, width = sig.shape
    steps = rows // SUB
    modes = rates.shape[0]
    tiles = width // LANES
    piece = width // GROUP
    halves = piece // LANES
    me = lax.axis_index("ctx")
    count = lax.axis_size("ctx")
    outer = count // GROUP
    half = outer // 2
    g = me // GROUP
    l = me - g * GROUP
    chip = l // 2
    core = l - chip * 2

    order = chip + chip // 2 - 2 * (chip // 3)

    def member(k):
        pair = k // 2
        hop = 2 - pair + 3 * (pair // 2) - 2 * (pair // 3)
        return 2 * lax.rem(chip + hop, CHIPS) + lax.rem(core + 1 + k, 2)

    taps_load = pltpu.make_async_copy(taps_hbm, taps, load_sem.at[0])
    rates_load = pltpu.make_async_copy(rates_hbm, rates, load_sem.at[1])
    late_loads = [
        pltpu.make_async_copy(streams_hbm.at[0], streams.at[0], load_sem.at[2]),
        pltpu.make_async_copy(residues_hbm, residues, load_sem.at[3]),
        pltpu.make_async_copy(skip_hbm, skip, load_sem.at[4]),
    ]

    def piece_load(k):
        at = lanes(member(k), piece)
        return pltpu.make_async_copy(
            streams_hbm.at[pl.ds(1, 2), :, at], streams.at[pl.ds(1, 2), :, at], piece_sem.at[k]
        )

    taps_load.start()
    piece_load(0).start()
    rates_load.start()

    bar = pltpu.get_barrier_semaphore()

    def greet(ctx):
        pl.semaphore_signal(bar, inc=1, device_id={"ctx": ctx}, device_id_type=MESH)

    def along(other):
        return other * GROUP + l

    for k in range(1, GROUP):
        greet(g * GROUP + lax.rem(l + k, GROUP))

    first_half = g < half
    for k in range(1, outer):

        @pl.when((g + k < outer) & (first_half | (k == 1)))
        def _():
            greet(along(g + k))

    @pl.when(g > half)
    def _():
        greet(along(g - 1))

    greetings = (
        GROUP
        - 1
        + jnp.minimum(g, half)
        + jnp.where(g > half, 1, 0)
        + jnp.where((g >= half) & (g < outer - 1), 1, 0)
    )

    for k in range(1, GROUP):
        piece_load(k).start()
    for load in late_loads:
        load.start()

    perm = gather_rows(rows)
    sub_row = lax.broadcasted_iota(jnp.int32, (SUB, LANES), 0)
    sub_pos = sub_row.astype(F32) * float(steps)
    to_end = sub_pos - float(steps * (SUB - 1))

    def signal_of(k):
        p = member(k)
        at = lanes(p, piece)
        piece_load(k).wait()
        one, one_edge = featurize(perm, streams, taps, 1, at)
        two, two_edge = featurize(perm, streams, taps, 2, at)
        row = lax.broadcasted_iota(jnp.int32, (rows, piece), 0)
        sig[:, at] = jnp.where((row == 0) | (row == SUB), 0.0, one * two)
        edge_row = lax.broadcasted_iota(jnp.int32, (SUB, piece), 0)
        edges = jnp.where(edge_row < 4, one_edge, two_edge)
        edges = jnp.concatenate(
            [edges[:, h * LANES : h * LANES + LANES] for h in range(halves)], axis=0
        ).astype(BF16)
        edges_out[p] = edges
        sbuf[p, halves * modes :, :] = edges

    def state_of(k):
        p = member(k)
        for half in range(halves):
            at = lanes(p * halves + half)
            factor = [
                jnp.broadcast_to(decay[pl.ds(m, 1), at], (SUB, LANES)) for m in range(modes)
            ]
            held = [sig[0:SUB, at]] * modes
            for b in range(1, steps):
                x = sig[SUB * b : SUB * b + SUB, at]
                held = [h * f + x for h, f in zip(held, factor)]
            ends = []
            for m in range(modes):
                weight = jnp.exp(to_end * rates[pl.ds(m, 1), at])
                ends.append(jnp.sum(held[m] * weight, axis=0, keepdims=True))
            sbuf[p, half * modes : half * modes + modes, :] = jnp.concatenate(
                ends, axis=0
            ).astype(BF16)

    def first_send(k):
        to = member(k)
        return pltpu.make_async_remote_copy(
            src_ref=sbuf.at[to],
            dst_ref=abuf.at[l],
            send_sem=a_send,
            recv_sem=a_recv.at[l],
            device_id={"ctx": g * GROUP + to},
            device_id_type=MESH,
        )

    def halo_send(source, target, which):
        return pltpu.make_async_remote_copy(
            src_ref=source,
            dst_ref=target,
            send_sem=halo_sem.at[2 * which],
            recv_sem=halo_sem.at[2 * which + 1],
            device_id={"ctx": lax.rem(me + 1, count)},
            device_id_type=MESH,
        )

    taps_load.wait()
    signal_of(0)
    rates_load.wait()
    decay[...] = jnp.exp(-rates[...])

    def early_step(k, carry):
        state_of(k)
        signal_of(k + 1)
        return carry

    def send_step(k, carry):
        first_send(k).start()
        return carry

    def state_and_send(k, carry):
        state_of(k)
        first_send(k).start()
        signal_of(k + 1)
        return carry

    answer_at = LAST_ANSWER_AT - ANSWER_LESS * order
    lax.fori_loop(0, answer_at, early_step, 0)
    pl.semaphore_wait(bar, greetings)

    def tell_group(other, k):
        pl.semaphore_signal(
            groups_in.at[k - 1], inc=1, device_id={"ctx": along(other)}, device_id_type=MESH
        )

    for k in range(1, outer):

        @pl.when((k <= g) & (g - k < half))
        def _():
            tell_group(g - k, k)

    @pl.when((g > half) & (g < outer - 1))
    def _():
        tell_group(g - 1, 2)

    lax.fori_loop(0, answer_at, send_step, 0)
    lax.fori_loop(answer_at, GROUP - 2, state_and_send, 0)
    state_of(GROUP - 2)
    first_send(GROUP - 2).start()
    signal_of(GROUP - 1)
    state_of(GROUP - 1)
    abuf[l] = sbuf[l]

    @pl.when(g == half + 1)
    def _():
        pl.semaphore_wait(groups_in.at[1], 1)
        tell_group(half, 3)


    for load in late_loads:
        load.wait()

    def gate_step(p, carry):
        at = lanes(p, piece)
        features, edges = featurize(perm, streams, taps, 0, at)
        gate[:, at] = features
        gate_edges_out[p] = jnp.concatenate(
            [edges[:, h * LANES : h * LANES + LANES] for h in range(halves)], axis=0
        ).astype(BF16)
        return carry

    lax.fori_loop(0, GROUP, gate_step, 0, unroll=4)
    halo = halo_send(edges_out, edges_in, 0)
    gate_halo = halo_send(gate_edges_out, gate_edges_in, 1)

    @pl.when(l < GROUP - 1)
    def _():
        halo.start()
        gate_halo.start()

    @pl.when((l == 0) & (g < outer - 1))
    def _():
        @pl.when(first_half)
        def _():
            pl.semaphore_wait(groups_in.at[0], 1)

        pl.semaphore_signal(
            next_in, inc=1, device_id={"ctx": me + GROUP - 1}, device_id_type=MESH
        )

    def reach_step(c, carry):
        at = lanes(c)
        for m in range(modes):
            rate = rates[pl.ds(m, 1), at]
            lead = residues[pl.ds(m, 1), at] * decay[pl.ds(m, 1), at]
            reach[c, m] = lead * jnp.exp(-sub_pos * rate)
        return carry

    lax.fori_loop(0, tiles, reach_step, 0)

    def own_step(c, carry):
        at = lanes(c)
        factor = [jnp.broadcast_to(decay[pl.ds(m, 1), at], (SUB, LANES)) for m in range(modes)]
        weight = [jnp.broadcast_to(residues[pl.ds(m, 1), at], (SUB, LANES)) for m in range(modes)]
        direct = jnp.broadcast_to(skip[0:1, at], (SUB, LANES))
        held = None
        for b in range(steps):
            x = sig[SUB * b : SUB * b + SUB, at]
            held = [x] * modes if b == 0 else [h * f + x for h, f in zip(held, factor)]
            terms = direct * x
            for h, w in zip(held, weight):
                terms = terms + h * w
            base[SUB * b : SUB * b + SUB, at] = terms
        for m in range(modes):
            rate = rates[pl.ds(m, 1), at]
            begin = jnp.where(sub_row < 1, 0.0, pltpu.roll(held[m], 1, 0))
            for back_rows in (1, 2, 4):
                begin = begin + jnp.exp(rate * (-float(steps * back_rows))) * jnp.where(
                    sub_row < back_rows, 0.0, pltpu.roll(begin, back_rows, 0)
                )
            inner[c, m] = weight[m] * factor[m] * begin
        return carry

    early_tiles = EARLY_TILES - EARLY_LESS * order
    middle_tiles = jnp.minimum(tiles, early_tiles + jnp.where(g < half, FEW_MIDDLE, MIDDLE_TILES))
    lax.fori_loop(0, early_tiles, own_step, 0)

    @pl.when((l == GROUP - 1) & (g < outer - 1))
    def _():
        pl.semaphore_wait(next_in, 1)
        halo.start()
        gate_halo.start()

    for k in range(1, outer):

        @pl.when(k > g)
        def _():
            bbuf[k - 1] = jnp.zeros(bbuf.shape[1:], BF16)

    mine = [lanes(l * halves + half) for half in range(halves)]
    my_rates = [rates[:, at] for at in mine]
    my_weights = [edge_weights(taps, at) for at in mine]

    def power(n):
        return [jnp.exp(rate * (-float(n))) for rate in my_rates]

    def unpack(message):
        value = message.astype(F32)
        body = [value[h * modes : h * modes + modes] for h in range(halves)]
        edge = value[halves * modes :]
        return body, [edge[h * SUB : h * SUB + SUB] for h in range(halves)]

    def with_edge(body, first, second, own, before):
        done = []
        for h in range(halves):
            s = edge_signal(my_weights[h], own[h], before[h])
            done.append(body[h] + first[h] * s[0:1] + second[h] * s[1:2])
        return done

    chunk_decay = power(rows)
    to_first = power(rows - 1)
    to_second = power(rows - 2)
    others = pl.ds(0, GROUP - 1)

    def arrived(k):
        @pl.when(l != k)
        def _():
            pltpu.make_async_copy(sbuf.at[k], abuf.at[k], a_recv.at[k]).wait()

        return unpack(abuf[k])

    total, first_edge = arrived(0)
    first_body = total
    before = first_edge
    for k in range(1, GROUP):
        body, edge = arrived(k)
        body = with_edge(body, to_first, to_second, edge, before)
        for h in range(halves):
            full[k, h * modes : h * modes + modes, :] = body[h]
        total = [t * d + b for t, d, b in zip(total, chunk_decay, body)]
        before = edge
    group_edge = [jnp.where((sub_row & 3) < 2, a, b) for a, b in zip(first_edge, before)]
    tbuf[...] = jnp.concatenate(total + group_edge, axis=0).astype(BF16)

    def group_copy(k):
        return pltpu.make_async_remote_copy(
            src_ref=tbuf,
            dst_ref=bbuf.at[k - 1],
            send_sem=b_send.at[k - 1],
            recv_sem=b_recv.at[k - 1],
            device_id={"ctx": along(g + k)},
            device_id_type=MESH,
        )

    def group_send(k):
        @pl.when(g + k < outer)
        def _():
            waited = ((k == 1) & (l == 0)) | ((k == 2) & (g == half + 1))

            @pl.when((first_half | (k > 1)) & jnp.logical_not(waited))
            def _():
                pl.semaphore_wait(groups_in.at[k - 1], 1)

            group_copy(k).start()

    for k in range(1, outer):
        group_send(k)

    lax.fori_loop(early_tiles, middle_tiles, own_step, 0)

    one_up = power(-1)
    two_up = power(-2)

    def boost(own, before):
        done = []
        for h in range(halves):
            s = edge_signal(my_weights[h], own[h], before[h])
            done.append(one_up[h] * s[0:1] + two_up[h] * s[1:2])
        return done

    before = first_edge
    for k in range(1, GROUP):
        edge = unpack(abuf[k])[1]
        extra[k] = jnp.concatenate(boost(edge, before), axis=0)
        before = edge

    group_decay = power(rows * GROUP)
    group_first = power(rows * GROUP - 1)
    group_second = power(rows * GROUP - 2)
    held = [jnp.zeros((modes, LANES), F32)] * halves
    before = [jnp.zeros((SUB, LANES), F32)] * halves
    for k in range(outer - 1, 0, -1):

        @pl.when(k <= g)
        def _():
            pltpu.make_async_copy(tbuf, bbuf.at[k - 1], b_recv.at[k - 1]).wait()

        body, edge = unpack(bbuf[k - 1])
        body = with_edge(body, group_first, group_second, edge, before)
        held = [h * d + b for h, d, b in zip(held, group_decay, body)]
        before = edge
    def last_send(k):
        return pltpu.make_async_remote_copy(
            src_ref=hbuf.at[k],
            dst_ref=cbuf.at[l],
            send_sem=c_send,
            recv_sem=c_recv.at[l],
            device_id={"ctx": g * GROUP + k},
            device_id_type=MESH,
        )

    extra[0] = jnp.concatenate(boost(first_edge, before), axis=0)
    for k in range(GROUP):
        if k == 1:
            body = with_edge(first_body, to_first, to_second, first_edge, before)
        elif k > 1:
            body = [full[k - 1, h * modes : h * modes + modes, :] for h in range(halves)]
        if k > 0:
            held = [h * d + b for h, d, b in zip(held, chunk_decay, body)]
        hbuf[k] = (jnp.concatenate(held, axis=0) + extra[k]).astype(BF16)

        @pl.when(l != k)
        def _():
            last_send(k).start()

    cbuf[l] = hbuf[l]
    back = scatter_rows(rows)
    lax.fori_loop(middle_tiles, tiles, own_step, 0)

    @pl.when(me > 0)
    def _():
        halo.wait_recv()

    @pl.when(me == 0)
    def _():
        edges_in[...] = jnp.zeros_like(edges_in)

    def edge_step(p, carry):
        for h in range(halves):
            at = lanes(p * halves + h)
            part = slice(h * SUB, h * SUB + SUB)
            s = edge_signal(
                edge_weights(taps, at),
                edges_out[p].astype(F32)[part],
                edges_in[p].astype(F32)[part],
            )
            ahead = jnp.sum(residues[:, at] * jnp.exp(rates[:, at]), axis=0, keepdims=True)
            base[0:1, at] += skip[0:1, at] * s[0:1] - ahead * s[1:2]
            base[SUB : SUB + 1, at] += skip[0:1, at] * s[1:2]
        return carry

    lax.fori_loop(0, GROUP, edge_step, 0)

    @pl.when(me > 0)
    def _():
        gate_halo.wait_recv()

    @pl.when(me == 0)
    def _():
        gate_edges_in[...] = jnp.zeros_like(gate_edges_in)

    def gate_edge_step(p, carry):
        for h in range(halves):
            at = lanes(p * halves + h)
            part = slice(h * SUB, h * SUB + SUB)
            f = edge_features(
                [taps[j, 0:1, at] for j in range(3)],
                gate_edges_out[p].astype(F32)[part],
                gate_edges_in[p].astype(F32)[part],
            )
            gate[0:1, at] = f[0:1]
            gate[SUB : SUB + 1, at] = f[1:2]
        return carry

    lax.fori_loop(0, GROUP, gate_edge_step, 0)


    def mix_of(p, ready):
        entering[...] = cbuf[p].astype(F32)
        for half in range(halves):
            c = p * halves + half
            at = lanes(c)
            factor = [
                jnp.broadcast_to(decay[pl.ds(m, 1), at], (SUB, LANES)) for m in range(modes)
            ]
            term = [
                inner[c, m] + reach[c, m] * entering[pl.ds(half * modes + m, 1), :]
                for m in range(modes)
            ]
            column = []
            for b in range(steps):
                terms = base[SUB * b : SUB * b + SUB, at]
                for h in term:
                    terms = terms + h
                column.append(gate[SUB * b : SUB * b + SUB, at] * terms)
                if b < steps - 1:
                    term = [h * f for h, f in zip(term, factor)]
            ready[:, half * LANES : half * LANES + LANES] = jnp.concatenate(
                column, axis=0
            ).astype(BF16)

    def put_back(p, ready):
        out[:, lanes(p, piece)] = jnp.dot(
            back, ready[...], preferred_element_type=F32
        ).astype(BF16)

    def mix_next(k, ready, last_ready):
        p = member(k)
        pltpu.make_async_copy(hbuf.at[p], cbuf.at[p], c_recv.at[p]).wait()
        put_back(member(k + 1), last_ready)
        mix_of(p, ready)

    mix_of(l, ready_a)

    def mix_pair(j, carry):
        mix_next(GROUP - 2 - 2 * j, ready_b, ready_a)
        mix_next(GROUP - 3 - 2 * j, ready_a, ready_b)
        return carry

    lax.fori_loop(0, GROUP // 2 - 1, mix_pair, 0)
    mix_next(0, ready_b, ready_a)
    put_back(member(0), ready_b)

    @pl.when(me < count - 1)
    def _():
        halo.wait_send()
        gate_halo.wait_send()

    pltpu.make_async_copy(sbuf.at[others], abuf.at[others], a_send).wait()
    pltpu.make_async_copy(hbuf.at[others], cbuf.at[others], c_send).wait()
    for k in range(1, outer):

        @pl.when(g + k < outer)
        def _():
            group_copy(k).wait_send()


def local(streams, short_filter, rates, residues, skip):
    _, rows, width = streams.shape
    modes = rates.shape[0]
    tiles = width // LANES
    halves = tiles // GROUP
    outer = lax.axis_size("ctx") // GROUP
    args = (streams, short_filter, rates, residues, skip[None, :])
    wide = pltpu.VMEM((rows, width), F32)
    per_mode = pltpu.VMEM((tiles, modes, SUB, LANES), F32)
    edges = pltpu.VMEM((GROUP, halves * SUB, LANES), BF16)
    body = halves * modes
    message = body + halves * SUB
    dma = pltpu.SemaphoreType.DMA
    return pl.pallas_call(
        kernel,
        out_shape=pltpu.VMEM((rows, width), BF16),
        in_specs=[pl.BlockSpec(memory_space=pltpu.HBM)] * len(args),
        out_specs=pl.BlockSpec(memory_space=pltpu.VMEM),
        scratch_shapes=[
            pltpu.VMEM(streams.shape, BF16),
            pltpu.VMEM(short_filter.shape, F32),
            pltpu.VMEM(rates.shape, F32),
            pltpu.VMEM(rates.shape, F32),
            pltpu.VMEM((1, width), F32),
            pltpu.VMEM(rates.shape, F32),
            wide,
            wide,
            wide,
            per_mode,
            per_mode,
            edges,
            edges,
            edges,
            edges,
            pltpu.VMEM((GROUP, message, LANES), BF16),
            pltpu.VMEM((GROUP, message, LANES), BF16),
            pltpu.VMEM((GROUP, body, LANES), F32),
            pltpu.VMEM((GROUP, body, LANES), F32),
            pltpu.VMEM((message, LANES), BF16),
            pltpu.VMEM((outer - 1, message, LANES), BF16),
            pltpu.VMEM((GROUP, body, LANES), BF16),
            pltpu.VMEM((GROUP, body, LANES), BF16),
            pltpu.VMEM((body, LANES), F32),
            pltpu.VMEM((rows, halves * LANES), BF16),
            pltpu.VMEM((rows, halves * LANES), BF16),
            dma((5,)),
            dma((GROUP,)),
            dma((4,)),
            pltpu.SemaphoreType.REGULAR((outer - 1,)),
            pltpu.SemaphoreType.REGULAR,
            dma,
            dma((GROUP,)),
            dma((outer - 1,)),
            dma((outer - 1,)),
            dma,
            dma((GROUP,)),
        ],
        compiler_params=pltpu.CompilerParams(
            collective_id=0, has_side_effects=True, vmem_limit_bytes=24 * 1024 * 1024
        ),
        name="mixer",
    )(*(pltpu.with_memory_space_constraint(a, pltpu.HBM) for a in args))


def solution(mesh):
    placed = (
        P(None, "ctx", "chan"),
        P(None, None, "chan"),
        P(None, "chan"),
        P(None, "chan"),
        P("chan"),
    )
    return jax.shard_map(
        local, mesh=mesh, in_specs=placed, out_specs=P("ctx", "chan"), check_vma=False
    )
```

```python
import jax
import jax.numpy as jnp
from jax import lax
from jax.experimental import pallas as pl
from jax.experimental.pallas import tpu as pltpu
from jax.sharding import PartitionSpec as P

MESH = pl.DeviceIdType.MESH
LANES = 128
LAST_ANSWER_AT = 6
ANSWER_LESS = 2
EARLY_TILES = 9
EARLY_LESS = 3
MIDDLE_TILES = 6
FEW_MIDDLE = 0
SUB = 8
GROUP = 8
CHIPS = GROUP // 2
F32 = jnp.float32
BF16 = jnp.bfloat16


def lanes(index, width=LANES):
    return pl.ds(pl.multiple_of(index * width, width), width)


def gather_rows(rows):
    steps = rows // SUB
    r = lax.broadcasted_iota(jnp.int32, (rows + 3 * SUB, rows), 0)
    t = lax.broadcasted_iota(jnp.int32, (rows + 3 * SUB, rows), 1)
    body = (r & (SUB - 1)) * steps + (r >> 3) - 2
    edge = (r & 3) + jnp.where((r & 3) < 2, 0, rows - 4)
    return (t == jnp.where(r < rows + 2 * SUB, body, edge)).astype(F32).astype(BF16)


def scatter_rows(rows):
    steps = rows // SUB
    t = lax.broadcasted_iota(jnp.int32, (rows, rows), 0)
    r = lax.broadcasted_iota(jnp.int32, (rows, rows), 1)
    return (t == (r & (SUB - 1)) * steps + (r >> 3)).astype(F32).astype(BF16)


def featurize(perm, streams, taps, stream, at):
    x = jnp.dot(perm, streams[stream, :, at], preferred_element_type=F32)
    rows = x.shape[0] - 3 * SUB
    features = (
        taps[0, pl.ds(stream, 1), at] * x[2 * SUB : 2 * SUB + rows]
        + taps[1, pl.ds(stream, 1), at] * x[SUB : SUB + rows]
        + taps[2, pl.ds(stream, 1), at] * x[:rows]
    )
    return features, x[2 * SUB + rows :]


def edge_features(weights, own, before):
    row = lax.broadcasted_iota(jnp.int32, own.shape, 0)
    one_back = jnp.where((row & 1) == 0, pltpu.roll(before, 5, 0), pltpu.roll(own, 1, 0))
    return weights[0] * own + weights[1] * one_back + weights[2] * pltpu.roll(before, 6, 0)


def edge_signal(weights, own, before):
    features = edge_features(weights, own, before)
    return features * pltpu.roll(features, 4, 0)


def edge_weights(taps, at):
    row = lax.broadcasted_iota(jnp.int32, (SUB, LANES), 0)
    return [jnp.where(row < 4, taps[j, 1:2, at], taps[j, 2:3, at]) for j in range(3)]


def kernel(
    streams_hbm,
    taps_hbm,
    rates_hbm,
    residues_hbm,
    skip_hbm,
    out,
    streams,
    taps,
    rates,
    residues,
    skip,
    decay,
    sig,
    gate,
    base,
    inner,
    reach,
    edges_out,
    edges_in,
    gate_edges_out,
    gate_edges_in,
    sbuf,
    abuf,
    full,
    extra,
    tbuf,
    bbuf,
    hbuf,
    cbuf,
    entering,
    ready_a,
    ready_b,
    load_sem,
    piece_sem,
    halo_sem,
    groups_in,
    next_in,
    a_send,
    a_recv,
    b_send,
    b_recv,
    c_send,
    c_recv,
):
    rows, width = sig.shape
    steps = rows // SUB
    modes = rates.shape[0]
    tiles = width // LANES
    piece = width // GROUP
    halves = piece // LANES
    me = lax.axis_index("ctx")
    count = lax.axis_size("ctx")
    outer = count // GROUP
    half = outer // 2
    g = me // GROUP
    l = me - g * GROUP
    chip = l // 2
    core = l - chip * 2

    def chip_at(place):
        return place + place // 2 - 2 * (place // 3)

    order = chip_at(chip)

    def member(k):
        pair = k // 2
        down = CHIPS - 1 - pair
        place = down - jnp.where(down <= order, 1, 0)
        place = jnp.where(order == CHIPS - 1, jnp.where(pair == 0, 0, down), place)
        other = jnp.where(pair == CHIPS - 1, chip, chip_at(place))
        return 2 * other + lax.rem(core + 1 + k, 2)

    def mix_member(n):
        up = jnp.maximum(n - 2, 0) // 2
        place = up + jnp.where(up >= order, 1, 0)
        other = jnp.where(n < 2, chip, chip_at(place))
        return 2 * other + lax.rem(core + n, 2)

    taps_load = pltpu.make_async_copy(taps_hbm, taps, load_sem.at[0])
    rates_load = pltpu.make_async_copy(rates_hbm, rates, load_sem.at[1])
    late_loads = [
        pltpu.make_async_copy(streams_hbm.at[0], streams.at[0], load_sem.at[2]),
        pltpu.make_async_copy(residues_hbm, residues, load_sem.at[3]),
        pltpu.make_async_copy(skip_hbm, skip, load_sem.at[4]),
    ]

    def piece_load(k):
        at = lanes(member(k), piece)
        return pltpu.make_async_copy(
            streams_hbm.at[pl.ds(1, 2), :, at], streams.at[pl.ds(1, 2), :, at], piece_sem.at[k]
        )

    taps_load.start()
    piece_load(0).start()
    rates_load.start()

    bar = pltpu.get_barrier_semaphore()

    def greet(ctx):
        pl.semaphore_signal(bar, inc=1, device_id={"ctx": ctx}, device_id_type=MESH)

    def along(other):
        return other * GROUP + l

    for k in range(1, GROUP):
        greet(g * GROUP + lax.rem(l + k, GROUP))

    first_half = g < half
    for k in range(1, outer):

        @pl.when((g + k < outer) & (first_half | (k == 1)))
        def _():
            greet(along(g + k))

    @pl.when(g > half)
    def _():
        greet(along(g - 1))

    greetings = (
        GROUP
        - 1
        + jnp.minimum(g, half)
        + jnp.where(g > half, 1, 0)
        + jnp.where((g >= half) & (g < outer - 1), 1, 0)
    )

    for k in range(1, GROUP):
        piece_load(k).start()
    for load in late_loads:
        load.start()

    perm = gather_rows(rows)
    sub_row = lax.broadcasted_iota(jnp.int32, (SUB, LANES), 0)
    sub_pos = sub_row.astype(F32) * float(steps)
    to_end = sub_pos - float(steps * (SUB - 1))

    def signal_of(k):
        p = member(k)
        at = lanes(p, piece)
        one, one_edge = featurize(perm, streams, taps, 1, at)
        two, two_edge = featurize(perm, streams, taps, 2, at)
        product = one * two
        row = lax.broadcasted_iota(jnp.int32, (2 * SUB, piece), 0)
        sig[0 : 2 * SUB, at] = jnp.where((row == 0) | (row == SUB), 0.0, product[: 2 * SUB])
        sig[2 * SUB :, at] = product[2 * SUB :]
        edge_row = lax.broadcasted_iota(jnp.int32, (SUB, piece), 0)
        edges = jnp.where(edge_row < 4, one_edge, two_edge)
        edges = jnp.concatenate(
            [edges[:, h * LANES : h * LANES + LANES] for h in range(halves)], axis=0
        ).astype(BF16)
        edges_out[p] = edges
        sbuf[p, halves * modes :, :] = edges

    def state_of(k):
        p = member(k)
        for half in range(halves):
            at = lanes(p * halves + half)
            factor = [
                jnp.broadcast_to(decay[pl.ds(m, 1), at], (SUB, LANES)) for m in range(modes)
            ]
            held = [sig[0:SUB, at]] * modes
            for b in range(1, steps):
                x = sig[SUB * b : SUB * b + SUB, at]
                held = [h * f + x for h, f in zip(held, factor)]
            ends = []
            for m in range(modes):
                weight = jnp.exp(to_end * rates[pl.ds(m, 1), at])
                ends.append(jnp.sum(held[m] * weight, axis=0, keepdims=True))
            sbuf[p, half * modes : half * modes + modes, :] = jnp.concatenate(
                ends, axis=0
            ).astype(BF16)

    def first_send(k):
        to = member(k)
        return pltpu.make_async_remote_copy(
            src_ref=sbuf.at[to],
            dst_ref=abuf.at[l],
            send_sem=a_send,
            recv_sem=a_recv.at[l],
            device_id={"ctx": g * GROUP + to},
            device_id_type=MESH,
        )

    def halo_send(source, target, which):
        return pltpu.make_async_remote_copy(
            src_ref=source,
            dst_ref=target,
            send_sem=halo_sem.at[2 * which],
            recv_sem=halo_sem.at[2 * which + 1],
            device_id={"ctx": lax.rem(me + 1, count)},
            device_id_type=MESH,
        )

    taps_load.wait()
    piece_load(0).wait()
    signal_of(0)
    rates_load.wait()
    decay[...] = jnp.exp(-rates[...])

    def early_step(k, carry):
        piece_load(k + 1).wait()
        state_of(k)
        signal_of(k + 1)
        return carry

    def send_step(k, carry):
        first_send(k).start()
        return carry

    def state_and_send(k, carry):
        piece_load(k + 1).wait()
        state_of(k)
        signal_of(k + 1)
        first_send(k).start()
        return carry

    answer_at = LAST_ANSWER_AT - ANSWER_LESS * order
    lax.fori_loop(0, answer_at, early_step, 0)
    pl.semaphore_wait(bar, greetings)

    def tell_group(other, k):
        pl.semaphore_signal(
            groups_in.at[k - 1], inc=1, device_id={"ctx": along(other)}, device_id_type=MESH
        )

    for k in range(1, outer):

        @pl.when((k <= g) & (g - k < half))
        def _():
            tell_group(g - k, k)

    @pl.when((g > half) & (g < outer - 1))
    def _():
        tell_group(g - 1, 2)

    lax.fori_loop(0, answer_at, send_step, 0)
    lax.fori_loop(answer_at, GROUP - 2, state_and_send, 0)
    state_of(GROUP - 2)
    first_send(GROUP - 2).start()
    piece_load(GROUP - 1).wait()
    signal_of(GROUP - 1)
    state_of(GROUP - 1)
    abuf[l] = sbuf[l]

    @pl.when(g == half + 1)
    def _():
        pl.semaphore_wait(groups_in.at[1], 1)
        tell_group(half, 3)


    for load in late_loads:
        load.wait()

    def gate_step(p, carry):
        at = lanes(p, piece)
        features, edges = featurize(perm, streams, taps, 0, at)
        gate[:, at] = features
        gate_edges_out[p] = jnp.concatenate(
            [edges[:, h * LANES : h * LANES + LANES] for h in range(halves)], axis=0
        ).astype(BF16)
        return carry

    lax.fori_loop(0, GROUP, gate_step, 0, unroll=4)
    halo = halo_send(edges_out, edges_in, 0)
    gate_halo = halo_send(gate_edges_out, gate_edges_in, 1)

    @pl.when(l < GROUP - 1)
    def _():
        halo.start()
        gate_halo.start()

    @pl.when((l == 0) & (g < outer - 1))
    def _():
        @pl.when(first_half)
        def _():
            pl.semaphore_wait(groups_in.at[0], 1)

        pl.semaphore_signal(
            next_in, inc=1, device_id={"ctx": me + GROUP - 1}, device_id_type=MESH
        )

    def reach_step(c, carry):
        at = lanes(c)
        for m in range(modes):
            rate = rates[pl.ds(m, 1), at]
            lead = residues[pl.ds(m, 1), at] * decay[pl.ds(m, 1), at]
            reach[c, m] = lead * jnp.exp(-sub_pos * rate)
        return carry

    lax.fori_loop(0, tiles, reach_step, 0)

    def own_step(c, carry):
        at = lanes(c)
        factor = [jnp.broadcast_to(decay[pl.ds(m, 1), at], (SUB, LANES)) for m in range(modes)]
        weight = [jnp.broadcast_to(residues[pl.ds(m, 1), at], (SUB, LANES)) for m in range(modes)]
        direct = jnp.broadcast_to(skip[0:1, at], (SUB, LANES))
        held = None
        for b in range(steps):
            x = sig[SUB * b : SUB * b + SUB, at]
            held = [x] * modes if b == 0 else [h * f + x for h, f in zip(held, factor)]
            terms = direct * x
            for h, w in zip(held, weight):
                terms = terms + h * w
            base[SUB * b : SUB * b + SUB, at] = terms
        for m in range(modes):
            rate = rates[pl.ds(m, 1), at]
            begin = jnp.where(sub_row < 1, 0.0, pltpu.roll(held[m], 1, 0))
            for back_rows in (1, 2, 4):
                begin = begin + jnp.exp(rate * (-float(steps * back_rows))) * jnp.where(
                    sub_row < back_rows, 0.0, pltpu.roll(begin, back_rows, 0)
                )
            inner[c, m] = weight[m] * factor[m] * begin
        return carry

    early_tiles = EARLY_TILES - EARLY_LESS * order
    middle_tiles = jnp.minimum(tiles, early_tiles + jnp.where(g < half, FEW_MIDDLE, MIDDLE_TILES))
    lax.fori_loop(0, early_tiles, own_step, 0)

    @pl.when((l == GROUP - 1) & (g < outer - 1))
    def _():
        pl.semaphore_wait(next_in, 1)
        halo.start()
        gate_halo.start()

    for k in range(1, outer):

        @pl.when(k > g)
        def _():
            bbuf[k - 1] = jnp.zeros(bbuf.shape[1:], BF16)

    mine = [lanes(l * halves + half) for half in range(halves)]
    my_rates = [rates[:, at] for at in mine]
    my_weights = [edge_weights(taps, at) for at in mine]

    def power(n):
        return [jnp.exp(rate * (-float(n))) for rate in my_rates]

    def unpack(message):
        value = message.astype(F32)
        body = [value[h * modes : h * modes + modes] for h in range(halves)]
        edge = value[halves * modes :]
        return body, [edge[h * SUB : h * SUB + SUB] for h in range(halves)]

    def with_edge(body, first, second, own, before):
        done = []
        for h in range(halves):
            s = edge_signal(my_weights[h], own[h], before[h])
            done.append(body[h] + first[h] * s[0:1] + second[h] * s[1:2])
        return done

    chunk_decay = power(rows)
    to_first = power(rows - 1)
    to_second = power(rows - 2)
    others = pl.ds(0, GROUP - 1)

    def arrived(k):
        @pl.when(l != k)
        def _():
            pltpu.make_async_copy(sbuf.at[k], abuf.at[k], a_recv.at[k]).wait()

        return unpack(abuf[k])

    total, first_edge = arrived(0)
    first_body = total
    before = first_edge
    for k in range(1, GROUP):
        body, edge = arrived(k)
        body = with_edge(body, to_first, to_second, edge, before)
        for h in range(halves):
            full[k, h * modes : h * modes + modes, :] = body[h]
        total = [t * d + b for t, d, b in zip(total, chunk_decay, body)]
        before = edge
    group_edge = [jnp.where((sub_row & 3) < 2, a, b) for a, b in zip(first_edge, before)]
    tbuf[...] = jnp.concatenate(total + group_edge, axis=0).astype(BF16)

    def group_copy(k):
        return pltpu.make_async_remote_copy(
            src_ref=tbuf,
            dst_ref=bbuf.at[k - 1],
            send_sem=b_send.at[k - 1],
            recv_sem=b_recv.at[k - 1],
            device_id={"ctx": along(g + k)},
            device_id_type=MESH,
        )

    def group_send(k):
        @pl.when(g + k < outer)
        def _():
            waited = ((k == 1) & (l == 0)) | ((k == 2) & (g == half + 1))

            @pl.when((first_half | (k > 1)) & jnp.logical_not(waited))
            def _():
                pl.semaphore_wait(groups_in.at[k - 1], 1)

            group_copy(k).start()

    for k in range(1, outer):
        group_send(k)

    lax.fori_loop(early_tiles, middle_tiles, own_step, 0)

    one_up = power(-1)
    two_up = power(-2)

    def boost(own, before):
        done = []
        for h in range(halves):
            s = edge_signal(my_weights[h], own[h], before[h])
            done.append(one_up[h] * s[0:1] + two_up[h] * s[1:2])
        return done

    before = first_edge
    for k in range(1, GROUP):
        edge = unpack(abuf[k])[1]
        extra[k] = jnp.concatenate(boost(edge, before), axis=0)
        before = edge

    group_decay = power(rows * GROUP)
    group_first = power(rows * GROUP - 1)
    group_second = power(rows * GROUP - 2)
    held = [jnp.zeros((modes, LANES), F32)] * halves
    before = [jnp.zeros((SUB, LANES), F32)] * halves
    for k in range(outer - 1, 0, -1):

        @pl.when(k <= g)
        def _():
            pltpu.make_async_copy(tbuf, bbuf.at[k - 1], b_recv.at[k - 1]).wait()

        body, edge = unpack(bbuf[k - 1])
        body = with_edge(body, group_first, group_second, edge, before)
        held = [h * d + b for h, d, b in zip(held, group_decay, body)]
        before = edge
    def last_send(k):
        return pltpu.make_async_remote_copy(
            src_ref=hbuf.at[k],
            dst_ref=cbuf.at[l],
            send_sem=c_send,
            recv_sem=c_recv.at[l],
            device_id={"ctx": g * GROUP + k},
            device_id_type=MESH,
        )

    extra[0] = jnp.concatenate(boost(first_edge, before), axis=0)
    for k in range(GROUP):
        if k == 1:
            body = with_edge(first_body, to_first, to_second, first_edge, before)
        elif k > 1:
            body = [full[k - 1, h * modes : h * modes + modes, :] for h in range(halves)]
        if k > 0:
            held = [h * d + b for h, d, b in zip(held, chunk_decay, body)]
        hbuf[k] = (jnp.concatenate(held, axis=0) + extra[k]).astype(BF16)

        @pl.when(l != k)
        def _():
            last_send(k).start()

    cbuf[l] = hbuf[l]
    back = scatter_rows(rows)
    lax.fori_loop(middle_tiles, tiles, own_step, 0)

    @pl.when(me > 0)
    def _():
        halo.wait_recv()

    @pl.when(me == 0)
    def _():
        edges_in[...] = jnp.zeros_like(edges_in)

    def edge_step(p, carry):
        for h in range(halves):
            at = lanes(p * halves + h)
            part = slice(h * SUB, h * SUB + SUB)
            s = edge_signal(
                edge_weights(taps, at),
                edges_out[p].astype(F32)[part],
                edges_in[p].astype(F32)[part],
            )
            ahead = jnp.sum(residues[:, at] * jnp.exp(rates[:, at]), axis=0, keepdims=True)
            base[0:1, at] += skip[0:1, at] * s[0:1] - ahead * s[1:2]
            base[SUB : SUB + 1, at] += skip[0:1, at] * s[1:2]
        return carry

    lax.fori_loop(0, GROUP, edge_step, 0)

    @pl.when(me > 0)
    def _():
        gate_halo.wait_recv()

    @pl.when(me == 0)
    def _():
        gate_edges_in[...] = jnp.zeros_like(gate_edges_in)

    def gate_edge_step(p, carry):
        for h in range(halves):
            at = lanes(p * halves + h)
            part = slice(h * SUB, h * SUB + SUB)
            f = edge_features(
                [taps[j, 0:1, at] for j in range(3)],
                gate_edges_out[p].astype(F32)[part],
                gate_edges_in[p].astype(F32)[part],
            )
            gate[0:1, at] = f[0:1]
            gate[SUB : SUB + 1, at] = f[1:2]
        return carry

    lax.fori_loop(0, GROUP, gate_edge_step, 0)


    def mix_of(p, ready):
        entering[...] = cbuf[p].astype(F32)
        for half in range(halves):
            c = p * halves + half
            at = lanes(c)
            factor = [
                jnp.broadcast_to(decay[pl.ds(m, 1), at], (SUB, LANES)) for m in range(modes)
            ]
            term = [
                inner[c, m] + reach[c, m] * entering[pl.ds(half * modes + m, 1), :]
                for m in range(modes)
            ]
            column = []
            for b in range(steps):
                sums = list(term)
                while len(sums) > 1:
                    sums = [x + y for x, y in zip(sums[::2], sums[1::2])]
                terms = base[SUB * b : SUB * b + SUB, at] + sums[0]
                column.append(gate[SUB * b : SUB * b + SUB, at] * terms)
                if b < steps - 1:
                    term = [h * f for h, f in zip(term, factor)]
            ready[:, half * LANES : half * LANES + LANES] = jnp.concatenate(
                column, axis=0
            ).astype(BF16)

    def put_back(p, ready):
        out[:, lanes(p, piece)] = jnp.dot(
            back, ready[...], preferred_element_type=F32
        ).astype(BF16)

    def mix_next(n, ready, last_ready):
        p = mix_member(n)
        pltpu.make_async_copy(hbuf.at[p], cbuf.at[p], c_recv.at[p]).wait()
        put_back(mix_member(n - 1), last_ready)
        mix_of(p, ready)

    mix_of(l, ready_a)

    def mix_pair(j, carry):
        mix_next(2 * j + 1, ready_b, ready_a)
        mix_next(2 * j + 2, ready_a, ready_b)
        return carry

    lax.fori_loop(0, GROUP // 2 - 1, mix_pair, 0)
    mix_next(GROUP - 1, ready_b, ready_a)
    put_back(mix_member(GROUP - 1), ready_b)

    @pl.when(me < count - 1)
    def _():
        halo.wait_send()
        gate_halo.wait_send()

    pltpu.make_async_copy(sbuf.at[others], abuf.at[others], a_send).wait()
    pltpu.make_async_copy(hbuf.at[others], cbuf.at[others], c_send).wait()
    for k in range(1, outer):

        @pl.when(g + k < outer)
        def _():
            group_copy(k).wait_send()


def local(streams, short_filter, rates, residues, skip):
    _, rows, width = streams.shape
    modes = rates.shape[0]
    tiles = width // LANES
    halves = tiles // GROUP
    outer = lax.axis_size("ctx") // GROUP
    args = (streams, short_filter, rates, residues, skip[None, :])
    wide = pltpu.VMEM((rows, width), F32)
    per_mode = pltpu.VMEM((tiles, modes, SUB, LANES), F32)
    edges = pltpu.VMEM((GROUP, halves * SUB, LANES), BF16)
    body = halves * modes
    message = body + halves * SUB
    dma = pltpu.SemaphoreType.DMA
    return pl.pallas_call(
        kernel,
        out_shape=pltpu.VMEM((rows, width), BF16),
        in_specs=[pl.BlockSpec(memory_space=pltpu.HBM)] * len(args),
        out_specs=pl.BlockSpec(memory_space=pltpu.VMEM),
        scratch_shapes=[
            pltpu.VMEM(streams.shape, BF16),
            pltpu.VMEM(short_filter.shape, F32),
            pltpu.VMEM(rates.shape, F32),
            pltpu.VMEM(rates.shape, F32),
            pltpu.VMEM((1, width), F32),
            pltpu.VMEM(rates.shape, F32),
            wide,
            wide,
            wide,
            per_mode,
            per_mode,
            edges,
            edges,
            edges,
            edges,
            pltpu.VMEM((GROUP, message, LANES), BF16),
            pltpu.VMEM((GROUP, message, LANES), BF16),
            pltpu.VMEM((GROUP, body, LANES), F32),
            pltpu.VMEM((GROUP, body, LANES), F32),
            pltpu.VMEM((message, LANES), BF16),
            pltpu.VMEM((outer - 1, message, LANES), BF16),
            pltpu.VMEM((GROUP, body, LANES), BF16),
            pltpu.VMEM((GROUP, body, LANES), BF16),
            pltpu.VMEM((body, LANES), F32),
            pltpu.VMEM((rows, halves * LANES), BF16),
            pltpu.VMEM((rows, halves * LANES), BF16),
            dma((5,)),
            dma((GROUP,)),
            dma((4,)),
            pltpu.SemaphoreType.REGULAR((outer - 1,)),
            pltpu.SemaphoreType.REGULAR,
            dma,
            dma((GROUP,)),
            dma((outer - 1,)),
            dma((outer - 1,)),
            dma,
            dma((GROUP,)),
        ],
        compiler_params=pltpu.CompilerParams(
            collective_id=0, has_side_effects=True, vmem_limit_bytes=24 * 1024 * 1024
        ),
        name="mixer",
    )(*(pltpu.with_memory_space_constraint(a, pltpu.HBM) for a in args))


def solution(mesh):
    placed = (
        P(None, "ctx", "chan"),
        P(None, None, "chan"),
        P(None, "chan"),
        P(None, "chan"),
        P("chan"),
    )
    return jax.shard_map(
        local, mesh=mesh, in_specs=placed, out_specs=P("ctx", "chan"), check_vma=False
    )
```

```python
import jax
import jax.numpy as jnp
from jax import lax
from jax.experimental import pallas as pl
from jax.experimental.pallas import tpu as pltpu
from jax.sharding import PartitionSpec as P

MESH = pl.DeviceIdType.MESH
LANES = 128
LAST_ANSWER_AT = 6
ANSWER_LESS = 2
EARLY_TILES = 9
EARLY_LESS = 3
MIDDLE_TILES = 6
FEW_MIDDLE = 0
SUB = 8
GROUP = 8
CHIPS = GROUP // 2
F32 = jnp.float32
BF16 = jnp.bfloat16


def lanes(index, width=LANES):
    return pl.ds(pl.multiple_of(index * width, width), width)


def gather_rows(rows):
    steps = rows // SUB
    r = lax.broadcasted_iota(jnp.int32, (rows + 3 * SUB, rows), 0)
    t = lax.broadcasted_iota(jnp.int32, (rows + 3 * SUB, rows), 1)
    body = (r & (SUB - 1)) * steps + (r >> 3) - 2
    edge = (r & 3) + jnp.where((r & 3) < 2, 0, rows - 4)
    return (t == jnp.where(r < rows + 2 * SUB, body, edge)).astype(F32).astype(BF16)


def scatter_rows(rows):
    steps = rows // SUB
    t = lax.broadcasted_iota(jnp.int32, (rows, rows), 0)
    r = lax.broadcasted_iota(jnp.int32, (rows, rows), 1)
    return (t == (r & (SUB - 1)) * steps + (r >> 3)).astype(F32).astype(BF16)


def featurize(perm, streams, taps, stream, at):
    x = jnp.dot(perm, streams[stream, :, at], preferred_element_type=F32)
    rows = x.shape[0] - 3 * SUB
    features = (
        taps[0, pl.ds(stream, 1), at] * x[2 * SUB : 2 * SUB + rows]
        + taps[1, pl.ds(stream, 1), at] * x[SUB : SUB + rows]
        + taps[2, pl.ds(stream, 1), at] * x[:rows]
    )
    return features, x[2 * SUB + rows :]


def edge_features(weights, own, before):
    row = lax.broadcasted_iota(jnp.int32, own.shape, 0)
    one_back = jnp.where((row & 1) == 0, pltpu.roll(before, 5, 0), pltpu.roll(own, 1, 0))
    return weights[0] * own + weights[1] * one_back + weights[2] * pltpu.roll(before, 6, 0)


def edge_signal(weights, own, before):
    features = edge_features(weights, own, before)
    return features * pltpu.roll(features, 4, 0)


def row_sums(values, row):
    def first(a, b):
        top = row < 4
        return jnp.where(top, a, b) + pltpu.roll(jnp.where(top, b, a), 4, 0)

    def merge(a, b, step):
        return jnp.where(
            (row & step) != 0, a + pltpu.roll(a, step, 0), b + pltpu.roll(b, SUB - step, 0)
        )

    odd = merge(first(values[3], values[7]), first(values[1], values[5]), 2)
    even = merge(first(values[2], values[6]), first(values[0], values[4]), 2)
    return merge(odd, even, 1)


def edge_weights(taps, at):
    row = lax.broadcasted_iota(jnp.int32, (SUB, LANES), 0)
    return [jnp.where(row < 4, taps[j, 1:2, at], taps[j, 2:3, at]) for j in range(3)]


def kernel(
    streams_hbm,
    taps_hbm,
    rates_hbm,
    residues_hbm,
    skip_hbm,
    out,
    streams,
    taps,
    rates,
    residues,
    skip,
    decay,
    sig,
    gate,
    base,
    inner,
    reach,
    edges_out,
    edges_in,
    gate_edges_out,
    gate_edges_in,
    sbuf,
    abuf,
    full,
    extra,
    tbuf,
    bbuf,
    hbuf,
    cbuf,
    entering,
    ready_a,
    ready_b,
    load_sem,
    piece_sem,
    halo_sem,
    groups_in,
    next_in,
    a_send,
    a_recv,
    b_send,
    b_recv,
    c_send,
    c_recv,
):
    rows, width = sig.shape
    steps = rows // SUB
    modes = rates.shape[0]
    tiles = width // LANES
    piece = width // GROUP
    halves = piece // LANES
    me = lax.axis_index("ctx")
    count = lax.axis_size("ctx")
    outer = count // GROUP
    half = outer // 2
    g = me // GROUP
    l = me - g * GROUP
    chip = l // 2
    core = l - chip * 2

    def chip_at(place):
        return place + place // 2 - 2 * (place // 3)

    order = chip_at(chip)

    def member(k):
        pair = k // 2
        down = CHIPS - 1 - pair
        place = down - jnp.where(down <= order, 1, 0)
        place = jnp.where(order == CHIPS - 1, jnp.where(pair == 0, 0, down), place)
        other = jnp.where(pair == CHIPS - 1, chip, chip_at(place))
        return 2 * other + lax.rem(core + 1 + k, 2)

    def mix_member(n):
        up = jnp.maximum(n - 2, 0) // 2
        place = up + jnp.where(up >= order, 1, 0)
        other = jnp.where(n < 2, chip, chip_at(place))
        return 2 * other + lax.rem(core + n, 2)

    taps_load = pltpu.make_async_copy(taps_hbm, taps, load_sem.at[0])
    rates_load = pltpu.make_async_copy(rates_hbm, rates, load_sem.at[1])
    late_loads = [
        pltpu.make_async_copy(streams_hbm.at[0], streams.at[0], load_sem.at[2]),
        pltpu.make_async_copy(residues_hbm, residues, load_sem.at[3]),
        pltpu.make_async_copy(skip_hbm, skip, load_sem.at[4]),
    ]

    def piece_load(k):
        at = lanes(member(k), piece)
        return pltpu.make_async_copy(
            streams_hbm.at[pl.ds(1, 2), :, at], streams.at[pl.ds(1, 2), :, at], piece_sem.at[k]
        )

    taps_load.start()
    piece_load(0).start()
    rates_load.start()

    bar = pltpu.get_barrier_semaphore()

    def greet(ctx):
        pl.semaphore_signal(bar, inc=1, device_id={"ctx": ctx}, device_id_type=MESH)

    def along(other):
        return other * GROUP + l

    for k in range(1, GROUP):
        greet(g * GROUP + lax.rem(l + k, GROUP))

    first_half = g < half
    for k in range(1, outer):

        @pl.when((g + k < outer) & (first_half | (k == 1)))
        def _():
            greet(along(g + k))

    @pl.when(g > half)
    def _():
        greet(along(g - 1))

    greetings = (
        GROUP
        - 1
        + jnp.minimum(g, half)
        + jnp.where(g > half, 1, 0)
        + jnp.where((g >= half) & (g < outer - 1), 1, 0)
    )

    for k in range(1, GROUP):
        piece_load(k).start()
    for load in late_loads:
        load.start()

    perm = gather_rows(rows)
    sub_row = lax.broadcasted_iota(jnp.int32, (SUB, LANES), 0)
    sub_pos = sub_row.astype(F32) * float(steps)
    to_end = sub_pos - float(steps * (SUB - 1))

    def signal_of(k):
        p = member(k)
        at = lanes(p, piece)
        one, one_edge = featurize(perm, streams, taps, 1, at)
        two, two_edge = featurize(perm, streams, taps, 2, at)
        product = one * two
        row = lax.broadcasted_iota(jnp.int32, (2 * SUB, piece), 0)
        sig[0 : 2 * SUB, at] = jnp.where((row == 0) | (row == SUB), 0.0, product[: 2 * SUB])
        sig[2 * SUB :, at] = product[2 * SUB :]
        edge_row = lax.broadcasted_iota(jnp.int32, (SUB, piece), 0)
        edges = jnp.where(edge_row < 4, one_edge, two_edge)
        edges = jnp.concatenate(
            [edges[:, h * LANES : h * LANES + LANES] for h in range(halves)], axis=0
        ).astype(BF16)
        edges_out[p] = edges
        sbuf[p, halves * modes :, :] = edges

    def state_of(k):
        p = member(k)
        for half in range(halves):
            at = lanes(p * halves + half)
            factor = [
                jnp.broadcast_to(decay[pl.ds(m, 1), at], (SUB, LANES)) for m in range(modes)
            ]
            held = [sig[0:SUB, at]] * modes
            for b in range(1, steps):
                x = sig[SUB * b : SUB * b + SUB, at]
                held = [h * f + x for h, f in zip(held, factor)]
            ends = []
            for m in range(modes):
                weight = jnp.exp(to_end * rates[pl.ds(m, 1), at])
                ends.append(held[m] * weight)
            sbuf[p, half * modes : half * modes + modes, :] = jnp.concatenate(
                [row_sums(ends[m : m + SUB], sub_row) for m in range(0, modes, SUB)], axis=0
            ).astype(BF16)

    def first_send(k):
        to = member(k)
        return pltpu.make_async_remote_copy(
            src_ref=sbuf.at[to],
            dst_ref=abuf.at[l],
            send_sem=a_send,
            recv_sem=a_recv.at[l],
            device_id={"ctx": g * GROUP + to},
            device_id_type=MESH,
        )

    def halo_send(source, target, which):
        return pltpu.make_async_remote_copy(
            src_ref=source,
            dst_ref=target,
            send_sem=halo_sem.at[2 * which],
            recv_sem=halo_sem.at[2 * which + 1],
            device_id={"ctx": lax.rem(me + 1, count)},
            device_id_type=MESH,
        )

    taps_load.wait()
    piece_load(0).wait()
    signal_of(0)
    rates_load.wait()
    decay[...] = jnp.exp(-rates[...])

    def early_step(k, carry):
        piece_load(k + 1).wait()
        state_of(k)
        signal_of(k + 1)
        return carry

    def send_step(k, carry):
        first_send(k).start()
        return carry

    def state_and_send(k, carry):
        piece_load(k + 1).wait()
        state_of(k)
        signal_of(k + 1)
        first_send(k).start()
        return carry

    answer_at = LAST_ANSWER_AT - ANSWER_LESS * order
    lax.fori_loop(0, answer_at, early_step, 0)
    pl.semaphore_wait(bar, greetings)

    def tell_group(other, k):
        pl.semaphore_signal(
            groups_in.at[k - 1], inc=1, device_id={"ctx": along(other)}, device_id_type=MESH
        )

    for k in range(1, outer):

        @pl.when((k <= g) & (g - k < half))
        def _():
            tell_group(g - k, k)

    @pl.when((g > half) & (g < outer - 1))
    def _():
        tell_group(g - 1, 2)

    lax.fori_loop(0, answer_at, send_step, 0)
    lax.fori_loop(answer_at, GROUP - 2, state_and_send, 0)
    state_of(GROUP - 2)
    first_send(GROUP - 2).start()
    piece_load(GROUP - 1).wait()
    signal_of(GROUP - 1)
    state_of(GROUP - 1)
    abuf[l] = sbuf[l]

    @pl.when(g == half + 1)
    def _():
        pl.semaphore_wait(groups_in.at[1], 1)
        tell_group(half, 3)


    for load in late_loads:
        load.wait()

    def gate_step(p, carry):
        at = lanes(p, piece)
        features, edges = featurize(perm, streams, taps, 0, at)
        gate[:, at] = features
        gate_edges_out[p] = jnp.concatenate(
            [edges[:, h * LANES : h * LANES + LANES] for h in range(halves)], axis=0
        ).astype(BF16)
        return carry

    lax.fori_loop(0, GROUP, gate_step, 0, unroll=4)
    halo = halo_send(edges_out, edges_in, 0)
    gate_halo = halo_send(gate_edges_out, gate_edges_in, 1)

    @pl.when(l < GROUP - 1)
    def _():
        halo.start()
        gate_halo.start()

    @pl.when((l == 0) & (g < outer - 1))
    def _():
        @pl.when(first_half)
        def _():
            pl.semaphore_wait(groups_in.at[0], 1)

        pl.semaphore_signal(
            next_in, inc=1, device_id={"ctx": me + GROUP - 1}, device_id_type=MESH
        )

    def reach_step(c, carry):
        at = lanes(c)
        for m in range(modes):
            rate = rates[pl.ds(m, 1), at]
            lead = residues[pl.ds(m, 1), at] * decay[pl.ds(m, 1), at]
            reach[c, m] = lead * jnp.exp(-sub_pos * rate)
        return carry

    lax.fori_loop(0, tiles, reach_step, 0)

    def own_step(c, carry):
        at = lanes(c)
        factor = [jnp.broadcast_to(decay[pl.ds(m, 1), at], (SUB, LANES)) for m in range(modes)]
        weight = [jnp.broadcast_to(residues[pl.ds(m, 1), at], (SUB, LANES)) for m in range(modes)]
        direct = jnp.broadcast_to(skip[0:1, at], (SUB, LANES))
        held = None
        for b in range(steps):
            x = sig[SUB * b : SUB * b + SUB, at]
            held = [x] * modes if b == 0 else [h * f + x for h, f in zip(held, factor)]
            terms = direct * x
            for h, w in zip(held, weight):
                terms = terms + h * w
            base[SUB * b : SUB * b + SUB, at] = terms
        for m in range(modes):
            rate = rates[pl.ds(m, 1), at]
            begin = jnp.where(sub_row < 1, 0.0, pltpu.roll(held[m], 1, 0))
            for back_rows in (1, 2, 4):
                begin = begin + jnp.exp(rate * (-float(steps * back_rows))) * jnp.where(
                    sub_row < back_rows, 0.0, pltpu.roll(begin, back_rows, 0)
                )
            inner[c, m] = weight[m] * factor[m] * begin
        return carry

    early_tiles = EARLY_TILES - EARLY_LESS * order
    middle_tiles = jnp.minimum(tiles, early_tiles + jnp.where(g < half, FEW_MIDDLE, MIDDLE_TILES))
    lax.fori_loop(0, early_tiles, own_step, 0)

    @pl.when((l == GROUP - 1) & (g < outer - 1))
    def _():
        pl.semaphore_wait(next_in, 1)
        halo.start()
        gate_halo.start()

    for k in range(1, outer):

        @pl.when(k > g)
        def _():
            bbuf[k - 1] = jnp.zeros(bbuf.shape[1:], BF16)

    mine = [lanes(l * halves + half) for half in range(halves)]
    my_rates = [rates[:, at] for at in mine]
    my_weights = [edge_weights(taps, at) for at in mine]

    def power(n):
        return [jnp.exp(rate * (-float(n))) for rate in my_rates]

    def unpack(message):
        value = message.astype(F32)
        body = [value[h * modes : h * modes + modes] for h in range(halves)]
        edge = value[halves * modes :]
        return body, [edge[h * SUB : h * SUB + SUB] for h in range(halves)]

    def with_edge(body, first, second, own, before):
        done = []
        for h in range(halves):
            s = edge_signal(my_weights[h], own[h], before[h])
            done.append(body[h] + first[h] * s[0:1] + second[h] * s[1:2])
        return done

    chunk_decay = power(rows)
    to_first = power(rows - 1)
    to_second = power(rows - 2)
    others = pl.ds(0, GROUP - 1)

    def arrived(k):
        @pl.when(l != k)
        def _():
            pltpu.make_async_copy(sbuf.at[k], abuf.at[k], a_recv.at[k]).wait()

        return unpack(abuf[k])

    total, first_edge = arrived(0)
    first_body = total
    before = first_edge
    for k in range(1, GROUP):
        body, edge = arrived(k)
        body = with_edge(body, to_first, to_second, edge, before)
        for h in range(halves):
            full[k, h * modes : h * modes + modes, :] = body[h]
        total = [t * d + b for t, d, b in zip(total, chunk_decay, body)]
        before = edge
    group_edge = [jnp.where((sub_row & 3) < 2, a, b) for a, b in zip(first_edge, before)]
    tbuf[...] = jnp.concatenate(total + group_edge, axis=0).astype(BF16)

    def group_copy(k):
        return pltpu.make_async_remote_copy(
            src_ref=tbuf,
            dst_ref=bbuf.at[k - 1],
            send_sem=b_send.at[k - 1],
            recv_sem=b_recv.at[k - 1],
            device_id={"ctx": along(g + k)},
            device_id_type=MESH,
        )

    def group_send(k):
        @pl.when(g + k < outer)
        def _():
            waited = ((k == 1) & (l == 0)) | ((k == 2) & (g == half + 1))

            @pl.when((first_half | (k > 1)) & jnp.logical_not(waited))
            def _():
                pl.semaphore_wait(groups_in.at[k - 1], 1)

            group_copy(k).start()

    for k in range(1, outer):
        group_send(k)

    lax.fori_loop(early_tiles, middle_tiles, own_step, 0)

    one_up = power(-1)
    two_up = power(-2)

    def boost(own, before):
        done = []
        for h in range(halves):
            s = edge_signal(my_weights[h], own[h], before[h])
            done.append(one_up[h] * s[0:1] + two_up[h] * s[1:2])
        return done

    before = first_edge
    for k in range(1, GROUP):
        edge = unpack(abuf[k])[1]
        extra[k] = jnp.concatenate(boost(edge, before), axis=0)
        before = edge

    group_decay = power(rows * GROUP)
    group_first = power(rows * GROUP - 1)
    group_second = power(rows * GROUP - 2)
    held = [jnp.zeros((modes, LANES), F32)] * halves
    before = [jnp.zeros((SUB, LANES), F32)] * halves
    for k in range(outer - 1, 0, -1):

        @pl.when(k <= g)
        def _():
            pltpu.make_async_copy(tbuf, bbuf.at[k - 1], b_recv.at[k - 1]).wait()

        body, edge = unpack(bbuf[k - 1])
        body = with_edge(body, group_first, group_second, edge, before)
        held = [h * d + b for h, d, b in zip(held, group_decay, body)]
        before = edge
    def last_send(k):
        return pltpu.make_async_remote_copy(
            src_ref=hbuf.at[k],
            dst_ref=cbuf.at[l],
            send_sem=c_send,
            recv_sem=c_recv.at[l],
            device_id={"ctx": g * GROUP + k},
            device_id_type=MESH,
        )

    extra[0] = jnp.concatenate(boost(first_edge, before), axis=0)
    for k in range(GROUP):
        if k == 1:
            body = with_edge(first_body, to_first, to_second, first_edge, before)
        elif k > 1:
            body = [full[k - 1, h * modes : h * modes + modes, :] for h in range(halves)]
        if k > 0:
            held = [h * d + b for h, d, b in zip(held, chunk_decay, body)]
        hbuf[k] = (jnp.concatenate(held, axis=0) + extra[k]).astype(BF16)

        @pl.when(l != k)
        def _():
            last_send(k).start()

    cbuf[l] = hbuf[l]
    back = scatter_rows(rows)
    lax.fori_loop(middle_tiles, tiles, own_step, 0)

    @pl.when(me > 0)
    def _():
        halo.wait_recv()

    @pl.when(me == 0)
    def _():
        edges_in[...] = jnp.zeros_like(edges_in)

    def edge_step(p, carry):
        for h in range(halves):
            at = lanes(p * halves + h)
            part = slice(h * SUB, h * SUB + SUB)
            s = edge_signal(
                edge_weights(taps, at),
                edges_out[p].astype(F32)[part],
                edges_in[p].astype(F32)[part],
            )
            ahead = jnp.sum(residues[:, at] * jnp.exp(rates[:, at]), axis=0, keepdims=True)
            base[0:1, at] += skip[0:1, at] * s[0:1] - ahead * s[1:2]
            base[SUB : SUB + 1, at] += skip[0:1, at] * s[1:2]
        return carry

    lax.fori_loop(0, GROUP, edge_step, 0)

    @pl.when(me > 0)
    def _():
        gate_halo.wait_recv()

    @pl.when(me == 0)
    def _():
        gate_edges_in[...] = jnp.zeros_like(gate_edges_in)

    def gate_edge_step(p, carry):
        for h in range(halves):
            at = lanes(p * halves + h)
            part = slice(h * SUB, h * SUB + SUB)
            f = edge_features(
                [taps[j, 0:1, at] for j in range(3)],
                gate_edges_out[p].astype(F32)[part],
                gate_edges_in[p].astype(F32)[part],
            )
            gate[0:1, at] = f[0:1]
            gate[SUB : SUB + 1, at] = f[1:2]
        return carry

    lax.fori_loop(0, GROUP, gate_edge_step, 0)


    def mix_of(p, ready):
        entering[...] = cbuf[p].astype(F32)
        for half in range(halves):
            c = p * halves + half
            at = lanes(c)
            factor = [
                jnp.broadcast_to(decay[pl.ds(m, 1), at], (SUB, LANES)) for m in range(modes)
            ]
            term = [
                inner[c, m] + reach[c, m] * entering[pl.ds(half * modes + m, 1), :]
                for m in range(modes)
            ]
            column = []
            for b in range(steps):
                sums = list(term)
                while len(sums) > 1:
                    sums = [x + y for x, y in zip(sums[::2], sums[1::2])]
                terms = base[SUB * b : SUB * b + SUB, at] + sums[0]
                column.append(gate[SUB * b : SUB * b + SUB, at] * terms)
                if b < steps - 1:
                    term = [h * f for h, f in zip(term, factor)]
            ready[:, half * LANES : half * LANES + LANES] = jnp.concatenate(
                column, axis=0
            ).astype(BF16)

    def put_back(p, ready):
        out[:, lanes(p, piece)] = jnp.dot(
            back, ready[...], preferred_element_type=F32
        ).astype(BF16)

    def mix_next(n, ready, last_ready):
        p = mix_member(n)
        pltpu.make_async_copy(hbuf.at[p], cbuf.at[p], c_recv.at[p]).wait()
        put_back(mix_member(n - 1), last_ready)
        mix_of(p, ready)

    mix_of(l, ready_a)

    def mix_pair(j, carry):
        mix_next(2 * j + 1, ready_b, ready_a)
        mix_next(2 * j + 2, ready_a, ready_b)
        return carry

    lax.fori_loop(0, GROUP // 2 - 1, mix_pair, 0)
    mix_next(GROUP - 1, ready_b, ready_a)
    put_back(mix_member(GROUP - 1), ready_b)

    @pl.when(me < count - 1)
    def _():
        halo.wait_send()
        gate_halo.wait_send()

    pltpu.make_async_copy(sbuf.at[others], abuf.at[others], a_send).wait()
    pltpu.make_async_copy(hbuf.at[others], cbuf.at[others], c_send).wait()
    for k in range(1, outer):

        @pl.when(g + k < outer)
        def _():
            group_copy(k).wait_send()


def local(streams, short_filter, rates, residues, skip):
    _, rows, width = streams.shape
    modes = rates.shape[0]
    tiles = width // LANES
    halves = tiles // GROUP
    outer = lax.axis_size("ctx") // GROUP
    args = (streams, short_filter, rates, residues, skip[None, :])
    wide = pltpu.VMEM((rows, width), F32)
    per_mode = pltpu.VMEM((tiles, modes, SUB, LANES), F32)
    edges = pltpu.VMEM((GROUP, halves * SUB, LANES), BF16)
    body = halves * modes
    message = body + halves * SUB
    dma = pltpu.SemaphoreType.DMA
    return pl.pallas_call(
        kernel,
        out_shape=pltpu.VMEM((rows, width), BF16),
        in_specs=[pl.BlockSpec(memory_space=pltpu.HBM)] * len(args),
        out_specs=pl.BlockSpec(memory_space=pltpu.VMEM),
        scratch_shapes=[
            pltpu.VMEM(streams.shape, BF16),
            pltpu.VMEM(short_filter.shape, F32),
            pltpu.VMEM(rates.shape, F32),
            pltpu.VMEM(rates.shape, F32),
            pltpu.VMEM((1, width), F32),
            pltpu.VMEM(rates.shape, F32),
            wide,
            wide,
            wide,
            per_mode,
            per_mode,
            edges,
            edges,
            edges,
            edges,
            pltpu.VMEM((GROUP, message, LANES), BF16),
            pltpu.VMEM((GROUP, message, LANES), BF16),
            pltpu.VMEM((GROUP, body, LANES), F32),
            pltpu.VMEM((GROUP, body, LANES), F32),
            pltpu.VMEM((message, LANES), BF16),
            pltpu.VMEM((outer - 1, message, LANES), BF16),
            pltpu.VMEM((GROUP, body, LANES), BF16),
            pltpu.VMEM((GROUP, body, LANES), BF16),
            pltpu.VMEM((body, LANES), F32),
            pltpu.VMEM((rows, halves * LANES), BF16),
            pltpu.VMEM((rows, halves * LANES), BF16),
            dma((5,)),
            dma((GROUP,)),
            dma((4,)),
            pltpu.SemaphoreType.REGULAR((outer - 1,)),
            pltpu.SemaphoreType.REGULAR,
            dma,
            dma((GROUP,)),
            dma((outer - 1,)),
            dma((outer - 1,)),
            dma,
            dma((GROUP,)),
        ],
        compiler_params=pltpu.CompilerParams(
            collective_id=0, has_side_effects=True, vmem_limit_bytes=24 * 1024 * 1024
        ),
        name="mixer",
    )(*(pltpu.with_memory_space_constraint(a, pltpu.HBM) for a in args))


def solution(mesh):
    placed = (
        P(None, "ctx", "chan"),
        P(None, None, "chan"),
        P(None, "chan"),
        P(None, "chan"),
        P("chan"),
    )
    return jax.shard_map(
        local, mesh=mesh, in_specs=placed, out_specs=P("ctx", "chan"), check_vma=False
    )
```
